128 devices in a mesh: expert: 32 (over y, x, core), dp: 4 (over z).
Axes of the slice: x: 4, y: 4, z: 4, core: 2. Of those that a mesh axis runs over, the one named last changes fastest.
Arguments:
- tokens: bfloat16 [16384, 2048], P(('expert', 'dp')), may hold values from -6 to 6
- expert_ids: int32 [16384, 8], P(('expert', 'dp')), may hold values from 0 to 63, all different within a row; in each aligned block of 128 rows (0 to 127, 128 to 255, ...) at most 24 rows name the same one
- gate_prob: float32 [16384, 8], P(('expert', 'dp')), may hold values from 0.05 to 0.3
- w_gate: bfloat16 [64, 2048, 384], P('expert', 'dp'), may hold values from -0.125 to 0.125
- w_up: bfloat16 [64, 2048, 384], P('expert', 'dp'), may hold values from -0.125 to 0.125
- w_down: bfloat16 [64, 384, 2048], P('expert', None, 'dp'), may hold values from -0.3125 to 0.3125
- grad_out: bfloat16 [16384, 2048], P(('expert', 'dp')), may hold values from -6 to 6
Outputs:
- mixed: bfloat16 [16384, 2048], P(('expert', 'dp'))
- grad_tokens: bfloat16 [16384, 2048], P(('expert', 'dp'))
- grad_gate: bfloat16 [64, 2048, 384], P('expert', 'dp')
- grad_up: bfloat16 [64, 2048, 384], P('expert', 'dp')
- grad_down: bfloat16 [64, 384, 2048], P('expert', None, 'dp')
The draws below stay inside these ranges and needn't reach their ends.
Inputs may be any that keep to these rules, and one draw needn't show every extreme that they name: `expert_ids`: each row names 8 different experts. In each aligned block of 128 rows (the rows of one device) no expert is named by more than 24 rows, a bound that some block reaches.
All inputs are finite; a program needn't handle non-finite values.
Results may differ from the reference program's by a relative error of at most 0.015.
Values may be sent and summed in bfloat16 or wider, within the bound.
A program may use at most 128 MiB of HBM per device.

```python
import math
import jax
import jax.numpy as jnp
import numpy as np
from jax import lax

D = 2048
FF = 384
TOPK = 8
TOK_DEV = 128
EXPERTS = 64
CAP = 24
DP_GROUPS = 4
TOKENS = 16384


def block_levels(own_key, extent, cuts, least, top_value):
    gain = 1.0
    for axis_at, shards_of in cuts:
        heights = jax.random.uniform(jax.random.fold_in(jax.random.fold_in(own_key, 6), axis_at), (shards_of,), jnp.float32, least / len(cuts), top_value / len(cuts))
        gain = gain * jnp.repeat(jnp.exp(heights), extent[axis_at] // shards_of).reshape((-1,) + (1,) * (len(extent) - 1 - axis_at))
    return gain


def routed_block(stream_key, own, number, rows, count, top, most, lean):
    ranking = jax.random.permutation(stream_key, count)
    crowded, ordinary = portions_of(count, rows * top, most, lean, True), portions_of(count, rows * top, most, lean, False)
    places = jnp.arange(count)

    def named(tallies, offset_by):
        used = int((tallies > 0).sum())
        fixed = max(1, used // 4)
        moved = fixed + (places - fixed + offset_by * (used - fixed)) % max(1, count - fixed)
        return jnp.zeros((count,), jnp.int32).at[ranking[jnp.where(places < fixed, places, moved)]].set(jnp.asarray(tallies, jnp.int32))

    tallies = jnp.where(number % 4 == 0, named(crowded, number // 4), named(ordinary, number - number // 4 - 1))
    mixed = jax.random.permutation(jax.random.fold_in(own, 3), count)
    giver, taker = mixed[0:count // 2 * 2:2], mixed[1:count // 2 * 2:2]
    slack = jnp.minimum(tallies[giver] - 1, most - tallies[taker]) // 2
    slack = jnp.where((giver == ranking[0]) | (taker == ranking[0]) | (tallies[taker] == 0), 0, jnp.maximum(slack, 0))
    moved = jax.random.randint(jax.random.fold_in(own, 4), (count // 2,), 0, 1 << 20) % (slack + 1)
    tallies = tallies.at[giver].add(-moved).at[taker].add(moved)
    members = jnp.searchsorted(jnp.cumsum(tallies), jnp.arange(rows * top), side="right").astype(jnp.int32)
    listing = members.reshape(top, rows).T
    listing = listing[jax.random.permutation(jax.random.fold_in(own, 1), rows)]
    offset_by = jax.random.randint(jax.random.fold_in(own, 2), (rows, 1), 0, top)
    return jnp.take_along_axis(listing, (jnp.arange(top)[None, :] + offset_by) % top, axis=1)


def portions_of(count, total, reach, slope, full):
    portions = [(1 << 20) // math.isqrt(rank ** slope) + 1 for rank in range(1, count + 1)]
    largest = reach if full else min(reach, max(-(-total // count), total * portions[0] // sum(portions)))
    least = 1 if total - largest >= count - 1 else 0
    holding, spare = [largest] + [least] * (count - 1), total - largest - least * (count - 1)
    while spare > 0:
        movable = [i for i in range(1, count) if holding[i] < largest] or [i for i in range(1, count) if holding[i] < reach]
        whole, left = sum([portions[i] for i in movable]), spare
        for i in movable:
            more = min(reach - holding[i], max(1, left * portions[i] // whole), spare)
            holding[i] = holding[i] + more
            spare = spare - more
    return np.array(holding)


def scatter_about(rng, extent, deviation, bound, cuts=(), held_as=jnp.bfloat16):
    factor_of = block_levels(rng, extent, cuts, -0.22, 0.18) if cuts else 1.0
    entries = jax.random.normal(rng, extent, jnp.float32) * deviation * factor_of
    return jnp.minimum(jnp.maximum(entries, -bound), bound).astype(held_as)


def setup_inputs(seed: int = 0) -> dict:
    key_list = jax.random.split(jax.random.key(seed), 8)
    tokens = scatter_about(key_list[0], (TOKENS, D), 1.0, 6.0, ((0, 128),))
    expert_ids_keys = jax.random.split(jax.random.fold_in(key_list[1], 1), TOKENS // TOK_DEV)
    expert_ids_turns = jax.random.permutation(jax.random.fold_in(key_list[1], 3), TOKENS // TOK_DEV)
    expert_ids = jax.vmap(lambda own, number: routed_block(jax.random.fold_in(key_list[1], 2), own, number, TOK_DEV, EXPERTS, TOPK, CAP, 2))(expert_ids_keys, expert_ids_turns).reshape((TOKENS, TOPK))
    gate_prob = jnp.clip(0.05 + 0.25 * jax.random.uniform(key_list[2], (TOKENS, TOPK), jnp.float32) ** block_levels(key_list[2], (TOKENS, TOPK), ((0, 128),), -0.2, 0.2), 0.05, 0.3)
    w_gate = scatter_about(key_list[3], (EXPERTS, D, FF), D ** -0.5, 0.125, ((0, 32), (1, 4)))
    w_up = scatter_about(key_list[4], (EXPERTS, D, FF), D ** -0.5, 0.125, ((0, 32), (1, 4)))
    w_down = scatter_about(key_list[5], (EXPERTS, FF, D), FF ** -0.5, 0.3125, ((0, 32), (2, 4)))
    grad_out = scatter_about(key_list[6], (TOKENS, D), 1.0, 6.0, ((0, 128),))
    return dict(tokens=tokens, expert_ids=expert_ids, gate_prob=gate_prob, w_gate=w_gate, w_up=w_up, w_down=w_down, grad_out=grad_out)


def silu_grad(a):
    s = jax.nn.sigmoid(a)
    return s * (1.0 + a * (1.0 - s))

def slot_positions(ids):
    flat = ids.reshape(-1)
    onehot = (flat[:, None] == jnp.arange(EXPERTS, dtype=jnp.int32)[None, :]).astype(jnp.int32)
    before = jnp.cumsum(onehot, axis=0) - onehot
    slot = lax.optimization_barrier(jnp.sum(before * onehot, axis=1))
    return (flat * CAP + slot).astype(jnp.int32)

def group_partial(left, right):
    blocks = left.shape[0] // CAP
    left_g = left.reshape(blocks // DP_GROUPS, DP_GROUPS, CAP, left.shape[1]).astype(jnp.float32)
    right_g = right.reshape(blocks // DP_GROUPS, DP_GROUPS, CAP, right.shape[1]).astype(jnp.float32)
    part = jnp.einsum('gdca,gdcb->dab', left_g, right_g).astype(jnp.bfloat16)
    return lax.optimization_barrier(jnp.sum(part.astype(jnp.float32), axis=0)).astype(jnp.bfloat16)

def reference(tokens, expert_ids, gate_prob, w_gate, w_up, w_down, grad_out):
    blocks = TOKENS // TOK_DEV
    ids = expert_ids.reshape(blocks, TOK_DEV, TOPK)
    pos = jax.vmap(slot_positions)(ids)
    block_ids = jnp.arange(blocks, dtype=jnp.int32)
    pair_tok = block_ids[:, None] * TOK_DEV + jnp.repeat(jnp.arange(TOK_DEV, dtype=jnp.int32), TOPK)[None, :]
    table = jnp.full((blocks, EXPERTS * CAP), TOKENS, jnp.int32)
    table = table.at[block_ids[:, None], pos].set(pair_tok.astype(jnp.int32))
    weights = jnp.zeros((blocks, EXPERTS * CAP), jnp.float32)
    weights = weights.at[block_ids[:, None], pos].set(gate_prob.reshape(blocks, TOK_DEV * TOPK))
    table = table.reshape(blocks, EXPERTS, CAP).transpose(1, 0, 2)
    weights = weights.reshape(blocks, EXPERTS, CAP).transpose(1, 0, 2)
    x_pad = jnp.concatenate([tokens, jnp.zeros((1, D), jnp.bfloat16)], axis=0)
    g_pad = jnp.concatenate([grad_out, jnp.zeros((1, D), jnp.bfloat16)], axis=0)

    def expert_step(carry, inputs):
        out_acc, dx_acc = carry
        rows_idx, row_prob, wg, wu, wd = inputs
        idx = rows_idx.reshape(-1).astype(jnp.int32)
        prob = row_prob.reshape(-1, 1)
        xs = x_pad[idx]
        a = jnp.dot(xs, wg, preferred_element_type=jnp.float32)
        b = jnp.dot(xs, wu, preferred_element_type=jnp.float32)
        hidden = (jax.nn.silu(a) * b).astype(jnp.bfloat16)
        y = jnp.dot(hidden, wd, preferred_element_type=jnp.float32).astype(jnp.bfloat16)
        out_acc = out_acc.at[idx].add(prob * y.astype(jnp.float32))
        dy = (prob * g_pad[idx].astype(jnp.float32)).astype(jnp.bfloat16)
        dh = jnp.dot(dy, wd.T, preferred_element_type=jnp.float32)
        da = (dh * b * silu_grad(a)).astype(jnp.bfloat16)
        db = (dh * jax.nn.silu(a)).astype(jnp.bfloat16)
        dx = (jnp.dot(da, wg.T, preferred_element_type=jnp.float32) + jnp.dot(db, wu.T, preferred_element_type=jnp.float32)).astype(jnp.bfloat16)
        dx_acc = dx_acc.at[idx].add(dx.astype(jnp.float32))
        gg = group_partial(xs, da)
        gu = group_partial(xs, db)
        gd = group_partial(hidden, dy)
        return ((out_acc, dx_acc), (gg, gu, gd))
    start = (jnp.zeros((TOKENS + 1, D), jnp.float32), jnp.zeros((TOKENS + 1, D), jnp.float32))
    (out_acc, dx_acc), (grad_gate, grad_up, grad_down) = lax.scan(expert_step, start, (table, weights, w_gate, w_up, w_down))
    mixed = out_acc[:TOKENS].astype(jnp.bfloat16)
    grad_tokens = dx_acc[:TOKENS].astype(jnp.bfloat16)
    return (mixed, grad_tokens, grad_gate, grad_up, grad_down)
```

```python
import jax
import jax.numpy as jnp
from jax import lax
from jax.experimental import pallas as pl
from jax.experimental.pallas import tpu as pltpu
from jax.sharding import PartitionSpec as P

MESH = pl.DeviceIdType.MESH
BF = jnp.bfloat16
F32 = jnp.float32
D = 2048
FF = 384
TOK = 128
CAP = 24
ROWS = 768
XW = D + 128
NT = (((1,), (1,)), ((), ()))
TN = (((0,), (0,)), ((), ()))
NN = (((1,), (0,)), ((), ()))


def dot(a, b, dims):
    return lax.dot_general(a, b, dims, preferred_element_type=F32)


def kernel(
    xm, g, wgate, wup, wdown,
    mixed, gtok, ggate, gup, gdown,
    xbuf, gbuf, ysib, qopp, qfull, popp, pfull,
    S, L, Wgu, Wd, YD, H, DAB, PW, P4, MB, YL, RB, zhg, zfg, zhd, zfd,
    a_send, a_recv, s_send, s_recv, w_send, w_recv, y_send, y_recv,
    q_send, q_recv, p_send, p_recv, z_send, z_recv, loc, ld, yl_sem,
):
    me = lax.axis_index("expert")
    z = lax.axis_index("dp")
    c = lax.rem(me, 2)
    x = lax.rem(me // 2, 4)
    y = me // 8
    sib = {"expert": me + 1 - 2 * c}
    zr, zl, zo = lax.rem(z + 1, 4), lax.rem(z + 3, 4), lax.rem(z + 2, 4)

    def pq(dp, dq):
        dx = dp + c * (dq - dp)
        dy = dq + c * (dp - dq)
        return {"expert": (lax.rem(y + dy, 4) * 4 + lax.rem(x + dx, 4)) * 2 + c}

    dev = {"P+": pq(1, 0), "P-": pq(3, 0), "Q+": pq(0, 1), "Q-": pq(0, 3), "S": sib, "Z+": {"dp": zr}, "Z-": {"dp": zl}}

    def slot(dp, dq):
        k0, k1 = dp * 4 + dq, dq * 4 + dp
        return k0 + c * (k1 - k0)

    barrier = pltpu.get_barrier_semaphore()
    for d in dev.values():
        pl.semaphore_signal(barrier, inc=1, device_id=d, device_id_type=MESH)
    pl.semaphore_wait(barrier, 7)

    pending = []

    def send(src, dst, ssem, rsem, to):
        cp = pltpu.make_async_remote_copy(
            src_ref=src, dst_ref=dst, send_sem=ssem, recv_sem=rsem, device_id=dev[to], device_id_type=MESH
        )
        cp.start()
        pending.append(cp)

    def arrived(dst, ssem, rsem):
        pltpu.make_async_remote_copy(
            src_ref=dst, dst_ref=dst, send_sem=ssem, recv_sem=rsem, device_id=dev["S"], device_id_type=MESH
        ).wait_recv()

    half = pl.ds(pl.multiple_of(c * TOK, TOK), TOK)
    other = pl.ds(pl.multiple_of((1 - c) * TOK, TOK), TOK)
    bufs = (xbuf, gbuf)
    counts = {"a": 0, "q": 0, "p": 0, "z": 0, "w": 0}

    def nxt(name):
        counts[name] += 1
        return counts[name] - 1

    def aidx(dp, dq, k):
        return (dp * 4 + dq) * 2 + k

    def blk(dp, dq, k):
        if dp == 0 and dq == 0:
            return (xm, g)[k]
        return bufs[k].at[slot(dp, dq), half, :]

    def push(dp, dq, k, to):
        ddp, ddq = dp, dq
        if to == "P+":
            ddp = (dp + 3) % 4
        elif to == "P-":
            ddp = (dp + 1) % 4
        elif to == "Q+":
            ddq = (dq + 3) % 4
        elif to == "Q-":
            ddq = (dq + 1) % 4
        send(blk(dp, dq, k), bufs[k].at[slot(ddp, ddq), half, :], a_send.at[nxt("a")], a_recv.at[aidx(ddp, ddq, k)], to)

    def push_sib(dp, dq, k):
        i = aidx(dp, dq, k)
        send(blk(dp, dq, k), bufs[k].at[slot(dp, dq), half, :], s_send.at[i], s_recv.at[i], "S")

    def take(dp, dq, k):
        i = aidx(dp, dq, k)
        arrived(bufs[k].at[slot(dp, dq), half, :], a_send.at[0], a_recv.at[i])

    def take_sib(dp, dq, k):
        i = aidx(dq, dp, k)
        arrived(bufs[k].at[slot(dp, dq), other, :], s_send.at[0], s_recv.at[i])

    for to in ("P+", "P-", "Q+", "Q-"):
        push(0, 0, 0, to)
    for to in ("P+", "P-", "Q+", "Q-"):
        push(0, 0, 1, to)

    def zrows(i):
        return pl.ds(pl.multiple_of(i * 512, 512), 512)

    wsrc = (wgate, wup, wdown)

    def wdst(k, i):
        if k == 2:
            return Wd.at[:, i]
        return Wgu.at[:, zrows(i), pl.ds(k * FF, FF)]

    for k in range(3):
        send(wsrc[k], wdst(k, z), w_send.at[nxt("w")], w_recv.at[k], "Z+")
        send(wsrc[k], wdst(k, z), w_send.at[nxt("w")], w_recv.at[3 + k], "Z-")
    own = [
        pltpu.make_async_copy(xm, xbuf.at[0, half, :], loc.at[0]),
        pltpu.make_async_copy(g, gbuf.at[0, half, :], loc.at[1]),
    ] + [pltpu.make_async_copy(wsrc[k], wdst(k, z), loc.at[2 + k]) for k in range(3)]
    for cp in own:
        cp.start()
    push_sib(0, 0, 0)
    push_sib(0, 0, 1)

    def w_fwd_gu():
        for k in (0, 1):
            arrived(wdst(k, zl), w_send.at[0], w_recv.at[k])
            arrived(wdst(k, zr), w_send.at[0], w_recv.at[3 + k])
        send(Wgu.at[0, zrows(zl)], Wgu.at[0, zrows(zl)], w_send.at[nxt("w")], w_recv.at[6], "Z+")
        send(Wgu.at[1, zrows(zr)], Wgu.at[1, zrows(zr)], w_send.at[nxt("w")], w_recv.at[7], "Z-")

    def w_fwd_d():
        arrived(wdst(2, zl), w_send.at[0], w_recv.at[2])
        arrived(wdst(2, zr), w_send.at[0], w_recv.at[5])
        send(Wd.at[0, zl], Wd.at[0, zl], w_send.at[nxt("w")], w_recv.at[8], "Z+")
        send(Wd.at[1, zr], Wd.at[1, zr], w_send.at[nxt("w")], w_recv.at[9], "Z-")

    def w_last():
        arrived(Wgu.at[0, zrows(zo)], w_send.at[0], w_recv.at[6])
        arrived(Wgu.at[1, zrows(zo)], w_send.at[0], w_recv.at[7])
        arrived(Wd.at[0, zo], w_send.at[0], w_recv.at[8])
        arrived(Wd.at[1, zo], w_send.at[0], w_recv.at[9])

    tri = (
        lax.broadcasted_iota(jnp.int32, (TOK, TOK), 0) <= lax.broadcasted_iota(jnp.int32, (TOK, TOK), 1)
    ).astype(F32).astype(BF)
    row8 = lax.broadcasted_iota(jnp.int32, (8, TOK), 0)
    slot_row = lax.broadcasted_iota(jnp.int32, (2 * CAP, TOK), 0).astype(F32)
    cf = c.astype(F32)
    e_own = (2 * me).astype(F32)
    e_sib = (2 * (me + 1 - 2 * c)).astype(F32)

    def load(chip, b):
        r = slot(*chip)
        for cp in load_copies(r, b):
            cp.start()

    def load_copies(r, b):
        return (
            pltpu.make_async_copy(xbuf.at[r, :, pl.ds(0, D)], L.at[pl.ds(b * 512, 256), :], ld.at[b, 0]),
            pltpu.make_async_copy(gbuf.at[r], L.at[pl.ds(b * 512 + 256, 256), :], ld.at[b, 1]),
            pltpu.make_async_copy(xbuf.at[r, pl.ds(0, 32), pl.ds(D, 128)], MB.at[b, 0], ld.at[b, 2]),
            pltpu.make_async_copy(xbuf.at[r, pl.ds(TOK, 32), pl.ds(D, 128)], MB.at[b, 1], ld.at[b, 3]),
        )

    def pick(chip, b):
        r = slot(*chip)
        for cp in load_copies(r, b):
            cp.wait()
        ids, prob = [], []
        for t in range(2):
            ids.append(MB[b, t, 0:8].astype(F32))
            prob.append(
                MB[b, t, 8:16].astype(F32) + (MB[b, t, 16:24].astype(F32) + MB[b, t, 24:32].astype(F32))
            )
        ids_c = jnp.where(c == 0, ids[0], ids[1])
        todo = [(ids[0], e_own), (ids[1], e_own), (ids[0], e_own + 1), (ids[1], e_own + 1), (ids_c, e_sib), (ids_c, e_sib + 1)]
        hit = jnp.zeros((8, TOK), F32)
        pv = []
        for j, (idv, e) in enumerate(todo):
            m = jnp.where(idv == e, 1.0, 0.0)
            if j < 4:
                pv.append(jnp.sum(m * prob[j % 2], axis=0, keepdims=True))
            hit = jnp.where(row8 == j, jnp.sum(m, axis=0, keepdims=True), hit)
        rank = dot(hit.astype(BF), tri, NN)
        key = jnp.where(hit > 0.5, rank - 1.0, -1000.0)
        p256, pown, psib = [], [], []
        for e in range(2):
            p0 = jnp.where(key[2 * e : 2 * e + 1] == slot_row, 1.0, 0.0)
            p1 = jnp.where(key[2 * e + 1 : 2 * e + 2] + CAP == slot_row, 1.0, 0.0)
            w = jnp.sum(p0 * pv[2 * e] + p1 * pv[2 * e + 1], axis=1, keepdims=True)
            at = pl.ds(pl.multiple_of(e * ROWS + r * 48, 16), 48)
            PW[at, :] = jnp.broadcast_to(w, (48, 128))
            p256.append(jnp.concatenate([p0, p1], axis=1))
            pown.append(jnp.where(c == 0, p0, p1))
            psib.append(jnp.where(key[4 + e : 5 + e] + CAP * cf == slot_row, 1.0, 0.0))
        P4[r] = jnp.concatenate(pown + psib, axis=0).astype(BF)
        pick_m = jnp.concatenate(p256, axis=0).astype(BF)

        def cols(n, _):
            cc = pl.ds(pl.multiple_of(n * 1024, 1024), 1024)
            for t in range(2):
                src = L[pl.ds(b * 512 + t * 256, 256), cc]
                got = dot(pick_m, src, NN).astype(BF)
                for e in range(2):
                    at = pl.ds(pl.multiple_of(t * 2 * ROWS + e * ROWS + r * 48, 16), 48)
                    S[at, cc] = got[e * 48 : e * 48 + 48]
            return 0

        lax.fori_loop(0, 2, cols, 0)

    def picks(chips):
        for i, chip in enumerate(chips):
            if i == 0:
                for k in range(2):
                    if chip != (0, 0) or k >= 0:
                        take_sib(chip[0], chip[1], k)
                load(chip, 0)
            if i + 1 < len(chips):
                for k in range(2):
                    take_sib(chips[i + 1][0], chips[i + 1][1], k)
                load(chips[i + 1], (i + 1) % 2)
            pick(chip, i % 2)

    take(3, 0, 0)
    push(3, 0, 0, "P+")
    push(3, 0, 0, "Q+")
    push(3, 0, 0, "Q-")
    take(1, 0, 0)
    push(1, 0, 0, "Q+")
    push(1, 0, 0, "Q-")
    take(1, 0, 1)
    push(1, 0, 1, "P-")
    push(1, 0, 1, "Q+")
    push(1, 0, 1, "Q-")
    take(3, 0, 1)
    push(3, 0, 1, "Q+")
    push(3, 0, 1, "Q-")

    def second_ring(dp):
        take(dp, 3, 0)
        push(dp, 3, 0, "Q+")
        take(dp, 1, 1)
        push(dp, 1, 1, "Q-")
        take(dp, 1, 0)
        take(dp, 3, 1)
        for dq in (3, 1):
            push_sib(dp, dq, 0)
            push_sib(dp, dq, 1)

    second_ring(0)
    for dp in (3, 1):
        push_sib(dp, 0, 0)
        push_sib(dp, 0, 1)
    for cp in own:
        cp.wait()
    picks([(0, 0)])
    w_fwd_gu()
    take(2, 0, 0)
    push(2, 0, 0, "Q+")
    push(2, 0, 0, "Q-")
    take(2, 0, 1)
    push(2, 0, 1, "Q+")
    push(2, 0, 1, "Q-")
    push_sib(2, 0, 0)
    push_sib(2, 0, 1)
    picks([(0, 3), (0, 1), (3, 0), (1, 0)])
    second_ring(3)
    second_ring(1)
    for k in range(2):
        take(0, 2, k)
        push_sib(0, 2, k)
    w_fwd_d()
    picks([(2, 0), (0, 2), (3, 3), (3, 1), (1, 3), (1, 1)])
    second_ring(2)
    for dp in (3, 1, 2):
        for k in range(2):
            take(dp, 2, k)
            push_sib(dp, 2, k)
    picks([(2, 3), (2, 1), (3, 2), (1, 2), (2, 2)])
    w_last()

    def forward(e):
        def tile(m, _):
            at = pl.ds(pl.multiple_of(m * 384, 384), 384)
            xs = S[pl.ds(pl.multiple_of(e * ROWS + m * 384, 384), 384), :]
            ab = dot(xs, Wgu[e], NN)
            gs_at = pl.ds(pl.multiple_of((2 + e) * ROWS + m * 384, 384), 384)
            dh = dot(S[gs_at, 0:512], Wd[e, 0], NT)
            for i in range(1, 4):
                dh = dh + dot(S[gs_at, i * 512 : i * 512 + 512], Wd[e, i], NT)
            w = PW[pl.ds(pl.multiple_of(e * ROWS + m * 384, 384), 384), 0:1]
            a, b = ab[:, :FF], ab[:, FF:]
            s = 1.0 / (1.0 + jnp.exp(-a))
            act = a * s
            dh = dh * w
            H[at, :] = (act * b * w).astype(BF)
            DAB[at, 0:FF] = (dh * b * s * (1.0 + a * (1.0 - s))).astype(BF)
            DAB[at, FF:] = (dh * act).astype(BF)
            return 0

        lax.fori_loop(0, 2, tile, 0)

    def outputs(e):
        def tile(m, _):
            at = pl.ds(pl.multiple_of(m * 384, 384), 384)
            for i in range(4):
                yv = dot(H[at, :], Wd[e, i], NN).astype(BF)
                YD[pl.ds(m * 8, 8), e * 48 : e * 48 + 48, i * 512 : i * 512 + 512] = yv.reshape(8, 48, 512)
            for i in range(4):
                dv = dot(DAB[at, :], Wgu[e, i * 512 : i * 512 + 512, :], NT).astype(BF)
                YD[pl.ds(m * 8, 8), e * 48 : e * 48 + 48, D + i * 512 : D + i * 512 + 512] = dv.reshape(8, 48, 512)
            return 0

        lax.fori_loop(0, 2, tile, 0)

    def weight_grads(e):
        def part(i, _):
            cc = zrows(i)
            xs = S[e * ROWS : e * ROWS + ROWS, cc]
            gs = S[(2 + e) * ROWS : (3 + e) * ROWS, cc]
            Wgu[e, cc, :] = dot(xs, DAB[...], TN).astype(BF)
            Wd[e, i] = dot(H[...], gs, TN).astype(BF)
            return 0

        lax.fori_loop(0, 4, part, 0)

    def zblk(e, i):
        return pl.ds(pl.multiple_of(i * 512, 512), 512)

    def zsend(src, dst, i, to):
        send(src, dst, z_send.at[i], z_recv.at[i], to)

    def z_first(e):
        base = e * 8
        lo = pl.ds(pl.multiple_of(zo * 512, 512), 256)
        hi = pl.ds(pl.multiple_of(zo * 512 + 256, 256), 256)
        zsend(Wgu.at[e, lo], zhg.at[e, 0], base + 0, "Z+")
        zsend(Wgu.at[e, hi], zhg.at[e, 1], base + 1, "Z-")
        zsend(Wd.at[e, zo, pl.ds(0, 192)], zhd.at[e, 0], base + 2, "Z+")
        zsend(Wd.at[e, zo, pl.ds(192, 192)], zhd.at[e, 1], base + 3, "Z-")

    def z_second(e):
        base = e * 8
        for i, (dst, rows) in enumerate(((zhg.at[e, 0], 0), (zhg.at[e, 1], 0), (zhd.at[e, 0], 0), (zhd.at[e, 1], 0))):
            arrived(dst, z_send.at[0], z_recv.at[base + i])

        def add(j, _):
            for i, (zz, off) in enumerate(((zr, 0), (zl, 256))):
                at = pl.ds(pl.multiple_of(zz * 512 + off + j * 32, 32), 32)
                Wgu[e, at, :] = (Wgu[e, at, :].astype(F32) + zhg[e, i, pl.ds(j * 32, 32), :].astype(F32)).astype(BF)
            return 0

        lax.fori_loop(0, 8, add, 0)

        def add_d(j, _):
            for i, (zz, off) in enumerate(((zr, 0), (zl, 192))):
                at = pl.ds(pl.multiple_of(off + j * 32, 32), 32)
                Wd[e, zz, at, :] = (Wd[e, zz, at, :].astype(F32) + zhd[e, i, pl.ds(j * 32, 32), :].astype(F32)).astype(BF)
            return 0

        lax.fori_loop(0, 6, add_d, 0)
        zsend(Wgu.at[e, zrows(zr)], zfg.at[e, 0], base + 4, "Z+")
        zsend(Wgu.at[e, zrows(zl)], zfg.at[e, 1], base + 5, "Z-")
        zsend(Wd.at[e, zr], zfd.at[e, 0], base + 6, "Z+")
        zsend(Wd.at[e, zl], zfd.at[e, 1], base + 7, "Z-")

    outs = []

    def z_third(e):
        base = e * 8
        for i, dst in enumerate((zfg.at[e, 0], zfg.at[e, 1], zfd.at[e, 0], zfd.at[e, 1])):
            arrived(dst, z_send.at[0], z_recv.at[base + 4 + i])

        def add(j, _):
            at = pl.ds(pl.multiple_of(z * 512 + j * 32, 32), 32)
            jj = pl.ds(pl.multiple_of(j * 32, 32), 32)
            Wgu[e, at, :] = (
                Wgu[e, at, :].astype(F32) + zfg[e, 0, jj, :].astype(F32) + zfg[e, 1, jj, :].astype(F32)
            ).astype(BF)
            return 0

        lax.fori_loop(0, 16, add, 0)

        def add_d(j, _):
            jj = pl.ds(pl.multiple_of(j * 32, 32), 32)
            Wd[e, z, jj, :] = (
                Wd[e, z, jj, :].astype(F32) + zfd[e, 0, jj, :].astype(F32) + zfd[e, 1, jj, :].astype(F32)
            ).astype(BF)
            return 0

        lax.fori_loop(0, 12, add_d, 0)
        for i, cp in enumerate(
            (
                (Wgu.at[e, zrows(z), pl.ds(0, FF)], ggate.at[e]),
                (Wgu.at[e, zrows(z), pl.ds(FF, FF)], gup.at[e]),
                (Wd.at[e, z], gdown.at[e]),
            )
        ):
            cp = pltpu.make_async_copy(cp[0], cp[1], loc.at[5 + e * 3 + i])
            cp.start()
            outs.append(cp)

    groups = (2, 1, 3, 0)
    order = (2, 1, 3, 0)
    chips = [(dp, dq) for dp in groups for dq in order]

    def yd_sends():
        for i, (dp, dq) in enumerate(chips):
            r = slot(dq, dp)
            send(YD.at[r], ysib.at[r], y_send.at[i], y_recv.at[i], "S")

    def yd_load(i):
        r = slot(*chips[i])
        return pltpu.make_async_copy(ysib.at[r], YL.at[i % 2], yl_sem.at[i % 2])

    def yd_start(i):
        r = slot(*chips[i])
        arrived(ysib.at[r], y_send.at[0], y_recv.at[i])
        yd_load(i).start()

    def cblk(gi, dq, k=0, n=1):
        row = dq * 256 + k * 128
        if gi == 0:
            return L, row, n * 128
        return S, (gi - 1) * 1024 + row, n * 128

    def cref(gi, dq, k=0, n=1):
        ref, row, cnt = cblk(gi, dq, k, n)
        return ref.at[pl.ds(row, cnt), :]

    def combine(gi):
        for j, dq in enumerate(order):
            i = gi * 4 + j
            if i == 0:
                yd_start(0)
            if i + 1 < 16:
                yd_start(i + 1)
            yd_load(i).wait()
            r = slot(*chips[i])
            ref, row, _ = cblk(gi, dq)
            pm = P4[r]

            def cols(n, _):
                cc = pl.ds(pl.multiple_of(n * 512, 512), 512)
                for k in range(2):
                    ck = pl.ds(pl.multiple_of(k * D + n * 512, 512), 512)
                    rows = jnp.concatenate([YD[r, :, ck], YL[i % 2, :, ck]], axis=0)
                    ref[row + k * 128 : row + k * 128 + 128, cc] = dot(pm, rows, TN).astype(BF)
                return 0

            lax.fori_loop(0, 4, cols, 0)

    def fetch(pairs):
        cps = [pltpu.make_async_copy(s, d, ld.at[0, i]) for i, (s, d) in enumerate(pairs)]
        for cp in cps:
            cp.start()
        for cp in cps:
            cp.wait()

    def accumulate(gi, dq, k, n, parts):
        ref, row, cnt = cblk(gi, dq, k, n)

        def add(j, _):
            at = pl.ds(pl.multiple_of(row + j * 16, 16), 16)
            total = ref[at, :].astype(F32)
            for off in parts:
                total = total + RB[pl.ds(pl.multiple_of(off + j * 16, 16), 16), :].astype(F32)
            ref[at, :] = total.astype(BF)
            return 0

        lax.fori_loop(0, cnt // 16, add, 0)

    def qsend(src, dst, gi, j, to):
        send(src, dst, q_send.at[gi * 4 + j], q_recv.at[gi * 4 + j], to)

    def q_first(gi):
        qsend(cref(gi, 2, 0), qopp.at[gi, 0], gi, 0, "Q+")
        qsend(cref(gi, 2, 1), qopp.at[gi, 1], gi, 1, "Q-")

    def q_second(gi):
        arrived(qopp.at[gi, 0], q_send.at[0], q_recv.at[gi * 4 + 0])
        arrived(qopp.at[gi, 1], q_send.at[0], q_recv.at[gi * 4 + 1])
        fetch([(qopp.at[gi, 0], RB.at[pl.ds(512, 128)]), (qopp.at[gi, 1], RB.at[pl.ds(640, 128)])])
        accumulate(gi, 1, 0, 1, (512,))
        qsend(cref(gi, 1, 0, 2), qfull.at[gi, 0], gi, 2, "Q+")
        accumulate(gi, 3, 1, 1, (640,))
        qsend(cref(gi, 3, 0, 2), qfull.at[gi, 1], gi, 3, "Q-")

    def psend(src, dst, j, to):
        send(src, dst, p_send.at[j], p_recv.at[j], to)

    def q_third(gi):
        arrived(qfull.at[gi, 0], q_send.at[0], q_recv.at[gi * 4 + 2])
        arrived(qfull.at[gi, 1], q_send.at[0], q_recv.at[gi * 4 + 3])
        fetch([(qfull.at[gi, 0], RB.at[pl.ds(0, 256)]), (qfull.at[gi, 1], RB.at[pl.ds(256, 256)])])
        accumulate(gi, 0, 0, 2, (0, 256))
        if gi == 0:
            psend(cref(0, 0, 0), popp.at[0], 0, "P+")
            psend(cref(0, 0, 1), popp.at[1], 1, "P-")
        elif gi == 1:
            arrived(popp.at[0], p_send.at[0], p_recv.at[0])
            fetch([(popp.at[0], RB.at[pl.ds(512, 128)])])
            accumulate(1, 0, 0, 1, (512,))
            psend(cref(1, 0, 0, 2), pfull.at[0], 2, "P+")
        elif gi == 2:
            arrived(popp.at[1], p_send.at[0], p_recv.at[1])
            fetch([(popp.at[1], RB.at[pl.ds(512, 128)])])
            accumulate(2, 0, 1, 1, (512,))
            psend(cref(2, 0, 0, 2), pfull.at[1], 3, "P-")
        else:
            arrived(pfull.at[0], p_send.at[0], p_recv.at[2])
            arrived(pfull.at[1], p_send.at[0], p_recv.at[3])
            fetch([(pfull.at[0], RB.at[pl.ds(0, 256)]), (pfull.at[1], RB.at[pl.ds(256, 256)])])
            accumulate(3, 0, 0, 2, (0, 256))
            for k, out in enumerate((mixed, gtok)):
                cp = pltpu.make_async_copy(cref(3, 0, k), out, loc.at[11 + k])
                cp.start()
                outs.append(cp)

    def end_sends():
        for cp in pending:
            cp.wait_send()
        pending.clear()

    forward(0)
    outputs(0)
    end_sends()
    weight_grads(0)
    z_first(0)
    forward(1)
    outputs(1)
    yd_sends()
    weight_grads(1)
    z_first(1)
    z_second(0)
    combine(0)
    q_first(0)
    combine(1)
    q_first(1)
    q_second(0)
    z_second(1)
    combine(2)
    q_first(2)
    q_second(1)
    q_third(0)
    combine(3)
    q_first(3)
    q_second(2)
    q_third(1)
    z_third(0)
    q_second(3)
    q_third(2)
    z_third(1)
    q_third(3)
    for cp in outs:
        cp.wait()
    end_sends()


def per_device(tokens, expert_ids, gate_prob, w_gate, w_up, w_down, grad_out):
    ids = expert_ids.T.astype(BF)
    p = gate_prob.T
    hi = lax.reduce_precision(p, 8, 7)
    rest = p - hi
    mid = lax.reduce_precision(rest, 8, 7)
    low = rest - mid
    meta = jnp.concatenate(
        [ids, hi.astype(BF), mid.astype(BF), low.astype(BF), jnp.zeros((96, TOK), BF)], axis=0
    )
    xm = jnp.concatenate([tokens, meta], axis=1)
    sds = jax.ShapeDtypeStruct
    hbm = pl.BlockSpec(memory_space=pl.ANY)
    dma = pltpu.SemaphoreType.DMA
    out_shape = (
        sds((TOK, D), BF),
        sds((TOK, D), BF),
        sds((2, 512, FF), BF),
        sds((2, 512, FF), BF),
        sds((2, FF, 512), BF),
        sds((16, 256, XW), BF),
        sds((16, 256, D), BF),
        sds((16, 96, 2 * D), BF),
        sds((4, 2, TOK, D), BF),
        sds((4, 2, 256, D), BF),
        sds((2, TOK, D), BF),
        sds((2, 256, D), BF),
    )
    scratch = [
        pltpu.VMEM((4 * ROWS, D), BF),
        pltpu.VMEM((1024, D), BF),
        pltpu.VMEM((2, D, 2 * FF), BF),
        pltpu.VMEM((2, 4, FF, 512), BF),
        pltpu.VMEM((16, 96, 2 * D), BF),
        pltpu.VMEM((ROWS, FF), BF),
        pltpu.VMEM((ROWS, 2 * FF), BF),
        pltpu.VMEM((2 * ROWS, 128), F32),
        pltpu.VMEM((16, 192, TOK), BF),
        pltpu.VMEM((2, 2, 32, 128), BF),
        pltpu.VMEM((2, 96, 2 * D), BF),
        pltpu.VMEM((768, D), BF),
        pltpu.VMEM((2, 2, 256, 2 * FF), BF),
        pltpu.VMEM((2, 2, 512, 2 * FF), BF),
        pltpu.VMEM((2, 2, 192, 512), BF),
        pltpu.VMEM((2, 2, FF, 512), BF),
        dma((30,)), dma((32,)), dma((32,)), dma((32,)),
        dma((10,)), dma((10,)), dma((16,)), dma((16,)),
        dma((16,)), dma((16,)), dma((4,)), dma((4,)),
        dma((16,)), dma((16,)), dma((13,)), dma((2, 4)), dma((2,)),
    ]
    res = pl.pallas_call(
        kernel,
        out_shape=out_shape,
        in_specs=[hbm] * 5,
        out_specs=[hbm] * len(out_shape),
        scratch_shapes=scratch,
        compiler_params=pltpu.CompilerParams(
            collective_id=0, has_side_effects=True, vmem_limit_bytes=63 * 1024 * 1024
        ),
    )(xm, grad_out, w_gate, w_up, w_down)
    return res[:5]


def solution(mesh):
    return jax.shard_map(
        per_device,
        mesh=mesh,
        in_specs=(
            P(("expert", "dp"), None),
            P(("expert", "dp"), None),
            P(("expert", "dp"), None),
            P("expert", "dp", None),
            P("expert", "dp", None),
            P("expert", None, "dp"),
            P(("expert", "dp"), None),
        ),
        out_specs=(
            P(("expert", "dp"), None),
            P(("expert", "dp"), None),
            P("expert", "dp", None),
            P("expert", "dp", None),
            P("expert", None, "dp"),
        ),
        check_vma=False,
    )
```

```python
import jax
import jax.numpy as jnp
from jax import lax
from jax.experimental import pallas as pl
from jax.experimental.pallas import tpu as pltpu
from jax.sharding import PartitionSpec as P

MESH = pl.DeviceIdType.MESH
BF = jnp.bfloat16
F32 = jnp.float32
D = 2048
FF = 384
TOK = 128
CAP = 24
KEEP = {"S": 6, "P": 6, "Q": 12, "Z": 8}
ROWS = 768
XW = D + 128
PLACES = [
    (0, 0), (0, 1), (0, 3), (1, 0), (3, 0), (0, 2), (2, 0),
    (2, 1), (2, 3), (1, 2), (3, 2), (2, 2),
    (1, 1), (1, 3), (3, 1), (3, 3),
]
NT = (((1,), (1,)), ((), ()))
TN = (((0,), (0,)), ((), ()))
NN = (((1,), (0,)), ((), ()))


def dot(a, b, dims):
    return lax.dot_general(a, b, dims, preferred_element_type=F32)


def kernel(
    tok, g, wgate, wup, wdown, eids, gprob,
    mixed, gtok, ggate, gup, gdown,
    xbuf, gbuf, ysib, qopp, qfull, popp, pfull,
    S, L, Wgu, Wd, YD, H, DAB, PW, P4, MB, MT, YL, RB, zhg, zfg, zhd, zfd, early,
    a_send, a_recv, s_send, s_recv, w_send, w_recv, y_send, y_recv,
    q_send, q_recv, p_send, p_recv, z_send, z_recv, loc, ld, yl_sem, m_send,
):
    me = lax.axis_index("expert")
    z = lax.axis_index("dp")
    c = lax.rem(me, 2)
    x = lax.rem(me // 2, 4)
    y = me // 8
    sib = {"expert": me + 1 - 2 * c}
    zr, zl, zo = lax.rem(z + 1, 4), lax.rem(z + 3, 4), lax.rem(z + 2, 4)

    def pq(dp, dq):
        dx = dp + c * (dq - dp)
        dy = dq + c * (dp - dq)
        return {"expert": (lax.rem(y + dy, 4) * 4 + lax.rem(x + dx, 4)) * 2 + c}

    dev = {"P+": pq(1, 0), "P-": pq(3, 0), "Q+": pq(0, 1), "Q-": pq(0, 3), "S": sib, "Z+": {"dp": zr}, "Z-": {"dp": zl}}

    def slot(dp, dq):
        k0, k1 = PLACES.index((dp, dq)), PLACES.index((dq, dp))
        return k0 + c * (k1 - k0)

    barrier = pltpu.get_barrier_semaphore()
    for d in dev.values():
        pl.semaphore_signal(barrier, inc=1, device_id=d, device_id_type=MESH)

    flying = {}

    def send(src, dst, ssem, rsem, to):
        cp = pltpu.make_async_remote_copy(
            src_ref=src, dst_ref=dst, send_sem=ssem, recv_sem=rsem, device_id=dev[to], device_id_type=MESH
        )
        line = flying.setdefault(to[0], [])
        while len(line) >= KEEP[to[0]]:
            line.pop(0).wait_send()
        cp.start()
        line.append(cp)

    def arrived(dst, ssem, rsem):
        pltpu.make_async_remote_copy(
            src_ref=dst, dst_ref=dst, send_sem=ssem, recv_sem=rsem, device_id=dev["S"], device_id_type=MESH
        ).wait_recv()

    half = pl.ds(pl.multiple_of(c * TOK, TOK), TOK)
    other = pl.ds(pl.multiple_of((1 - c) * TOK, TOK), TOK)
    bufs = (xbuf, gbuf)
    counts = {"a": 0, "m": 0}

    def nxt(name):
        counts[name] += 1
        return counts[name] - 1

    def aidx(dp, dq, k):
        return (dp * 4 + dq) * 2 + k

    def blk(dp, dq, k):
        return bufs[k].at[slot(dp, dq), half, :]

    def push(dp, dq, k, to):
        ddp, ddq = dp, dq
        if to == "P+":
            ddp = (dp + 3) % 4
        elif to == "P-":
            ddp = (dp + 1) % 4
        elif to == "Q+":
            ddq = (dq + 3) % 4
        elif to == "Q-":
            ddq = (dq + 1) % 4
        launch(dp, dq, k, slot(ddp, ddq), a_send, nxt("a"), a_recv.at[aidx(ddp, ddq, k)], to)

    def launch(dp, dq, k, r, ssem, i, rsem, to):
        dst = bufs[k].at[r, half, :]
        if dp or dq:
            send(blk(dp, dq, k), dst, ssem.at[i], rsem, to)
        elif k == 1:
            send(g, dst, ssem.at[i], rsem, to)
        else:
            send(tok, bufs[0].at[r, half, pl.ds(0, D)], ssem.at[i], rsem, to)
            send(MT, bufs[0].at[r, half, pl.ds(D, 128)], m_send.at[counts["m"]], rsem, to)
            counts["m"] += 1

    def push_sib(dp, dq, k):
        i = aidx(dp, dq, k)
        launch(dp, dq, k, slot(dp, dq), s_send, i, s_recv.at[i], "S")

    def take(dp, dq, k):
        i = aidx(dp, dq, k)
        arrived(bufs[k].at[slot(dp, dq), half, :], a_send.at[0], a_recv.at[i])

    def take_sib(dp, dq, k):
        i = aidx(dq, dp, k)
        arrived(bufs[k].at[slot(dp, dq), other, :], s_send.at[0], s_recv.at[i])

    eye = (
        lax.broadcasted_iota(jnp.int32, (TOK, TOK), 0) == lax.broadcasted_iota(jnp.int32, (TOK, TOK), 1)
    ).astype(F32).astype(BF)
    prob_in = gprob[...]
    hi = prob_in.astype(BF)
    mid = (prob_in - hi.astype(F32)).astype(BF)
    low = (prob_in - hi.astype(F32) - mid.astype(F32)).astype(BF)
    turned = [dot(v, eye, TN) for v in (eids[...].astype(F32).astype(BF), hi, mid, low)]
    MT[...] = jnp.concatenate(turned + [jnp.zeros((96, TOK), F32)], axis=0).astype(BF)
    pl.semaphore_wait(barrier, 7)

    def zrows(i):
        return pl.ds(pl.multiple_of(i * 512, 512), 512)

    wsrc = (wgate, wup, wdown)

    def wdst(e, k, i):
        if k == 2:
            return Wd.at[e, i]
        return Wgu.at[e, zrows(i), pl.ds(k * FF, FF)]

    own_w = [
        pltpu.make_async_copy(wsrc[k].at[e], wdst(e, k, z), loc.at[5 + 3 * e + k]) for e in range(2) for k in range(3)
    ]

    def w_own(e, kinds=(0, 1, 2)):
        for k in kinds:
            for j, to in enumerate(("Z+", "Z-")):
                wsend(wsrc[k].at[e], wdst(e, k, z), e * 10 + 3 * j + k, to)

    def wsend(src, dst, i, to):
        send(src, dst, w_send.at[i], w_recv.at[i], to)

    def w_parts(e, i):
        lo = pl.ds(pl.multiple_of(i * 512, 512), 256)
        hi = pl.ds(pl.multiple_of(i * 512 + 256, 256), 256)
        return (Wgu.at[e, lo], Wgu.at[e, hi], Wd.at[e, i, pl.ds(0, 192)], Wd.at[e, i, pl.ds(192, 192)])

    def w_fwd(e):
        for k in range(3):
            arrived(wdst(e, k, zl), w_send.at[0], w_recv.at[e * 10 + k])
            arrived(wdst(e, k, zr), w_send.at[0], w_recv.at[e * 10 + 3 + k])
        for j in range(4):
            part = w_parts(e, (zl, zr)[j % 2])[j]
            wsend(part, part, e * 10 + 6 + j, ("Z+", "Z-")[j % 2])

    def w_last(e):
        for j in range(4):
            arrived(w_parts(e, zo)[j], w_send.at[0], w_recv.at[e * 10 + 6 + j])

    for k in range(2):
        push(0, 0, k, "P+")
        push(0, 0, 1 - k, "P-")
        push(0, 0, k, "Q+")
        push(0, 0, 1 - k, "Q-")
        if k == 0:
            w_own(0)
            w_own(1, (0,))
    push_sib(0, 0, 0)
    push_sib(0, 0, 1)
    for cp in own_w:
        cp.start()

    tri = (
        lax.broadcasted_iota(jnp.int32, (TOK, TOK), 0) <= lax.broadcasted_iota(jnp.int32, (TOK, TOK), 1)
    ).astype(F32).astype(BF)
    row8 = lax.broadcasted_iota(jnp.int32, (8, TOK), 0)
    slot_row = lax.broadcasted_iota(jnp.int32, (2 * CAP, TOK), 0).astype(F32)
    cf = c.astype(F32)
    e_own = (2 * me).astype(F32)
    e_sib = (2 * (me + 1 - 2 * c)).astype(F32)

    def load(chip, b, buf):
        r = 0 if chip == (0, 0) else slot(*chip)
        for cp in load_copies(r, b, buf):
            cp.start()

    def load_copies(r, b, buf):
        if isinstance(r, int):
            r0 = b * 512
            mine, theirs = pl.ds(pl.multiple_of(r0 + c * TOK, TOK), TOK), pl.ds(pl.multiple_of(r0 + TOK - c * TOK, TOK), TOK)
            mine_g = pl.ds(pl.multiple_of(r0 + 256 + c * TOK, TOK), TOK)
            theirs_g = pl.ds(pl.multiple_of(r0 + 256 + TOK - c * TOK, TOK), TOK)
            few = pl.ds(pl.multiple_of((1 - c) * TOK, TOK), 32)
            return (
                pltpu.make_async_copy(tok, buf.at[mine, :], ld.at[b, 0]),
                pltpu.make_async_copy(xbuf.at[0, other, pl.ds(0, D)], buf.at[theirs, :], ld.at[b, 1]),
                pltpu.make_async_copy(g, buf.at[mine_g, :], ld.at[b, 2]),
                pltpu.make_async_copy(gbuf.at[0, other, :], buf.at[theirs_g, :], ld.at[b, 3]),
                pltpu.make_async_copy(MT.at[pl.ds(0, 32), :], MB.at[b, c], ld.at[b, 4]),
                pltpu.make_async_copy(xbuf.at[0, few, pl.ds(D, 128)], MB.at[b, 1 - c], ld.at[b, 5]),
            )
        return (
            pltpu.make_async_copy(xbuf.at[r, :, pl.ds(0, D)], buf.at[pl.ds(b * 512, 256), :], ld.at[b, 0]),
            pltpu.make_async_copy(gbuf.at[r], buf.at[pl.ds(b * 512 + 256, 256), :], ld.at[b, 1]),
            pltpu.make_async_copy(xbuf.at[r, pl.ds(0, 32), pl.ds(D, 128)], MB.at[b, 0], ld.at[b, 2]),
            pltpu.make_async_copy(xbuf.at[r, pl.ds(TOK, 32), pl.ds(D, 128)], MB.at[b, 1], ld.at[b, 3]),
        )

    def pick(chip, b, buf):
        r = 0 if chip == (0, 0) else slot(*chip)
        for cp in load_copies(r, b, buf):
            cp.wait()
        ids, prob = [], []
        for t in range(2):
            ids.append(MB[b, t, 0:8].astype(F32))
            prob.append(
                MB[b, t, 8:16].astype(F32) + (MB[b, t, 16:24].astype(F32) + MB[b, t, 24:32].astype(F32))
            )
        ids_c = jnp.where(c == 0, ids[0], ids[1])
        todo = [(ids[0], e_own), (ids[1], e_own), (ids[0], e_own + 1), (ids[1], e_own + 1), (ids_c, e_sib), (ids_c, e_sib + 1)]
        hit = jnp.zeros((8, TOK), F32)
        pv = []
        for j, (idv, e) in enumerate(todo):
            m = jnp.where(idv == e, 1.0, 0.0)
            if j < 4:
                pv.append(jnp.sum(m * prob[j % 2], axis=0, keepdims=True))
            hit = jnp.where(row8 == j, jnp.sum(m, axis=0, keepdims=True), hit)
        rank = dot(hit.astype(BF), tri, NN)
        key = jnp.where(hit > 0.5, rank - 1.0, -1000.0)
        p256, pown, psib = [], [], []
        for e in range(2):
            p0 = jnp.where(key[2 * e : 2 * e + 1] == slot_row, 1.0, 0.0)
            p1 = jnp.where(key[2 * e + 1 : 2 * e + 2] + CAP == slot_row, 1.0, 0.0)
            w = jnp.sum(p0 * pv[2 * e] + p1 * pv[2 * e + 1], axis=1, keepdims=True)
            at = pl.ds(pl.multiple_of(e * ROWS + r * 48, 16), 48)
            PW[at, :] = jnp.broadcast_to(w, (48, 128))
            p256.append(jnp.concatenate([p0, p1], axis=1))
            pown.append(jnp.where(c == 0, p0, p1))
            psib.append(jnp.where(key[4 + e : 5 + e] + CAP * cf == slot_row, 1.0, 0.0))
        P4[r] = jnp.concatenate(pown + psib, axis=0).astype(BF)
        pick_m = jnp.concatenate(p256, axis=0).astype(BF)

        def cols(n, _):
            cc = pl.ds(pl.multiple_of(n * 1024, 1024), 1024)
            for t in range(2):
                src = buf[pl.ds(b * 512 + t * 256, 256), cc]
                got = dot(pick_m, src, NN).astype(BF)
                for e in range(2):
                    at = pl.ds(pl.multiple_of(t * 2 * ROWS + e * ROWS + r * 48, 16), 48)
                    S[at, cc] = got[e * 48 : e * 48 + 48]
            return 0

        lax.fori_loop(0, 2, cols, 0)

    def picks(some, buf):
        for i, chip in enumerate(some):
            for j in (i, i + 1):
                if j < len(some) and (j > i or i == 0):
                    for k in range(2):
                        take_sib(*some[j], k)
                    load(some[j], j % 2, buf)
            pick(chip, i % 2, buf)

    def forward(e, tile):
        first, n = tile
        lo, cnt = first * 48, n * 48
        xs = S[e * ROWS + lo : e * ROWS + lo + cnt, :]
        ab = dot(xs, Wgu[e], NN)
        g0 = (2 + e) * ROWS + lo
        dh = dot(S[g0 : g0 + cnt, 0:512], Wd[e, 0], NT)
        for i in range(1, 4):
            dh = dh + dot(S[g0 : g0 + cnt, i * 512 : i * 512 + 512], Wd[e, i], NT)
        w = PW[e * ROWS + lo : e * ROWS + lo + cnt, 0:1]
        a, b = ab[:, :FF], ab[:, FF:]
        s = 1.0 / (1.0 + jnp.exp(-a))
        act = a * s
        dh = dh * w
        H[e, lo : lo + cnt, :] = (act * b * w).astype(BF)
        DAB[e, lo : lo + cnt, 0:FF] = (dh * b * s * (1.0 + a * (1.0 - s))).astype(BF)
        DAB[e, lo : lo + cnt, FF:] = (dh * act).astype(BF)

    def outputs(e, tile):
        first, n = tile
        lo, cnt = first * 48, n * 48
        for i in range(4):
            yv = dot(H[e, lo : lo + cnt, :], Wd[e, i], NN).astype(BF)
            YD[first : first + n, e * 48 : e * 48 + 48, i * 512 : i * 512 + 512] = yv.reshape(n, 48, 512)
        for i in range(4):
            dv = dot(DAB[e, lo : lo + cnt, :], Wgu[e, i * 512 : i * 512 + 512, :], NT).astype(BF)
            YD[first : first + n, e * 48 : e * 48 + 48, D + i * 512 : D + i * 512 + 512] = dv.reshape(n, 48, 512)

    def weight_grads(e):
        def part(j, _):
            i = lax.rem(z + j, 4)
            cc = zrows(i)
            xs = S[e * ROWS : e * ROWS + ROWS, cc]
            gs = S[(2 + e) * ROWS : (3 + e) * ROWS, cc]
            Wgu[e, cc, :] = dot(xs, DAB[e], TN).astype(BF)
            Wd[e, i] = dot(H[e], gs, TN).astype(BF)
            return 0

        lax.fori_loop(2, 3, part, 0)
        z_first(e)
        lax.fori_loop(3, 6, part, 0)

    def zsend(src, dst, i, to):
        send(src, dst, z_send.at[i], z_recv.at[i], to)

    def z_first(e):
        base = e * 8
        lo = pl.ds(pl.multiple_of(zo * 512, 512), 256)
        hi = pl.ds(pl.multiple_of(zo * 512 + 256, 256), 256)
        zsend(Wgu.at[e, lo], zhg.at[e, 0], base + 0, "Z+")
        zsend(Wgu.at[e, hi], zhg.at[e, 1], base + 1, "Z-")
        zsend(Wd.at[e, zo, pl.ds(0, 192)], zhd.at[e, 0], base + 2, "Z+")
        zsend(Wd.at[e, zo, pl.ds(192, 192)], zhd.at[e, 1], base + 3, "Z-")

    def z_second(e):
        base = e * 8
        for i, (dst, rows) in enumerate(((zhg.at[e, 0], 0), (zhg.at[e, 1], 0), (zhd.at[e, 0], 0), (zhd.at[e, 1], 0))):
            arrived(dst, z_send.at[0], z_recv.at[base + i])

        def add(j, _):
            for i, (zz, off) in enumerate(((zr, 0), (zl, 256))):
                at = pl.ds(pl.multiple_of(zz * 512 + off + j * 32, 32), 32)
                Wgu[e, at, :] = (Wgu[e, at, :].astype(F32) + zhg[e, i, pl.ds(j * 32, 32), :].astype(F32)).astype(BF)
            return 0

        lax.fori_loop(0, 8, add, 0)

        def add_d(j, _):
            for i, (zz, off) in enumerate(((zr, 0), (zl, 192))):
                at = pl.ds(pl.multiple_of(off + j * 32, 32), 32)
                Wd[e, zz, at, :] = (Wd[e, zz, at, :].astype(F32) + zhd[e, i, pl.ds(j * 32, 32), :].astype(F32)).astype(BF)
            return 0

        lax.fori_loop(0, 6, add_d, 0)
        zsend(Wgu.at[e, zrows(zr)], zfg.at[e, 0], base + 4, "Z+")
        zsend(Wgu.at[e, zrows(zl)], zfg.at[e, 1], base + 5, "Z-")
        zsend(Wd.at[e, zr], zfd.at[e, 0], base + 6, "Z+")
        zsend(Wd.at[e, zl], zfd.at[e, 1], base + 7, "Z-")

    outs = []

    def z_third(e):
        base = e * 8
        for i, dst in enumerate((zfg.at[e, 0], zfg.at[e, 1], zfd.at[e, 0], zfd.at[e, 1])):
            arrived(dst, z_send.at[0], z_recv.at[base + 4 + i])

        def add(j, _):
            at = pl.ds(pl.multiple_of(z * 512 + j * 32, 32), 32)
            jj = pl.ds(pl.multiple_of(j * 32, 32), 32)
            Wgu[e, at, :] = (
                Wgu[e, at, :].astype(F32) + zfg[e, 0, jj, :].astype(F32) + zfg[e, 1, jj, :].astype(F32)
            ).astype(BF)
            return 0

        lax.fori_loop(0, 16, add, 0)

        def add_d(j, _):
            jj = pl.ds(pl.multiple_of(j * 32, 32), 32)
            Wd[e, z, jj, :] = (
                Wd[e, z, jj, :].astype(F32) + zfd[e, 0, jj, :].astype(F32) + zfd[e, 1, jj, :].astype(F32)
            ).astype(BF)
            return 0

        lax.fori_loop(0, 12, add_d, 0)
        for i, cp in enumerate(
            (
                (Wgu.at[e, zrows(z), pl.ds(0, FF)], ggate.at[e]),
                (Wgu.at[e, zrows(z), pl.ds(FF, FF)], gup.at[e]),
                (Wd.at[e, z], gdown.at[e]),
            )
        ):
            cp = pltpu.make_async_copy(cp[0], cp[1], loc.at[5 + e * 3 + i])
            cp.start()
            outs.append(cp)

    far = [(2, 2), (1, 2), (3, 2), (0, 2)]
    near = [(2, 1), (2, 3), (0, 1), (0, 3), (1, 1), (1, 3), (3, 1), (3, 3)]
    mine = [(2, 0), (1, 0), (3, 0), (0, 0)]
    chips = far + near + mine

    def yd_sends(some):
        for i, (dp, dq) in enumerate(chips):
            if (dp, dq) in some:
                r = slot(dq, dp)
                send(YD.at[r], ysib.at[r], y_send.at[i], y_recv.at[i], "S")

    def yd_load(i):
        r = slot(*chips[i])
        return pltpu.make_async_copy(ysib.at[r], YL.at[i % 2], yl_sem.at[i % 2])

    def yd_start(i):
        r = slot(*chips[i])
        arrived(ysib.at[r], y_send.at[0], y_recv.at[i])
        yd_load(i).start()

    def cblk(dp, dq, k=0, n=1):
        if dq == 2:
            return L, dp * 256 + k * 128, n * 128
        if dp in (0, 2) and dq:
            return early, dp * 256 + dq // 2 * 256 + k * 128, n * 128
        return S, dp * 768 + {0: 0, 1: 256, 3: 512}[dq] + k * 128, n * 128

    def cref(dp, dq, k=0, n=1):
        ref, row, cnt = cblk(dp, dq, k, n)
        return ref.at[pl.ds(row, cnt), :]

    def combine(dp, dq, ahead=True):
        i = chips.index((dp, dq))
        if i + 1 < 16 and ahead:
            yd_start(i + 1)
        yd_load(i).wait()
        r = slot(dp, dq)
        ref, row, _ = cblk(dp, dq)
        pm = P4[r]

        def cols(n, _):
            cc = pl.ds(pl.multiple_of(n * 512, 512), 512)
            for k in range(2):
                ck = pl.ds(pl.multiple_of(k * D + n * 512, 512), 512)
                rows = jnp.concatenate([YD[r, :, ck], YL[i % 2, :, ck]], axis=0)
                ref[row + k * 128 : row + k * 128 + 128, cc] = dot(pm, rows, TN).astype(BF)
            return 0

        lax.fori_loop(0, 4, cols, 0)

    def fetch(pairs):
        cps = [pltpu.make_async_copy(s, d, ld.at[0, i]) for i, (s, d) in enumerate(pairs)]
        for cp in cps:
            cp.start()
        for cp in cps:
            cp.wait()

    def accumulate(dp, dq, k, n, parts):
        ref, row, cnt = cblk(dp, dq, k, n)

        def add(j, _):
            at = pl.ds(pl.multiple_of(row + j * 16, 16), 16)
            total = ref[at, :].astype(F32)
            for off in parts:
                total = total + RB[pl.ds(pl.multiple_of(off + j * 16, 16), 16), :].astype(F32)
            ref[at, :] = total.astype(BF)
            return 0

        lax.fori_loop(0, cnt // 16, add, 0)

    def qsend(src, dst, dp, j, to):
        send(src, dst, q_send.at[dp * 4 + j], q_recv.at[dp * 4 + j], to)

    def q_first(dp):
        qsend(cref(dp, 2, 0), qopp.at[dp, 0], dp, 0, "Q+")
        qsend(cref(dp, 2, 1), qopp.at[dp, 1], dp, 1, "Q-")

    def q_second(dp):
        arrived(qopp.at[dp, 0], q_send.at[0], q_recv.at[dp * 4 + 0])
        arrived(qopp.at[dp, 1], q_send.at[0], q_recv.at[dp * 4 + 1])
        fetch([(qopp.at[dp, 0], RB.at[pl.ds(512, 128)]), (qopp.at[dp, 1], RB.at[pl.ds(640, 128)])])
        accumulate(dp, 1, 0, 1, (512,))
        qsend(cref(dp, 1, 0, 2), qfull.at[dp, 0], dp, 2, "Q+")
        accumulate(dp, 3, 1, 1, (640,))
        qsend(cref(dp, 3, 0, 2), qfull.at[dp, 1], dp, 3, "Q-")

    def psend(src, dst, j, to):
        send(src, dst, p_send.at[j], p_recv.at[j], to)

    def q_third(dp):
        arrived(qfull.at[dp, 0], q_send.at[0], q_recv.at[dp * 4 + 2])
        arrived(qfull.at[dp, 1], q_send.at[0], q_recv.at[dp * 4 + 3])
        fetch([(qfull.at[dp, 0], RB.at[pl.ds(0, 256)]), (qfull.at[dp, 1], RB.at[pl.ds(256, 256)])])
        accumulate(dp, 0, 0, 2, (0, 256))
        if dp == 2:
            psend(cref(2, 0, 0), popp.at[0], 0, "P+")
            psend(cref(2, 0, 1), popp.at[1], 1, "P-")
        elif dp == 1:
            arrived(popp.at[0], p_send.at[0], p_recv.at[0])
            fetch([(popp.at[0], RB.at[pl.ds(512, 128)])])
            accumulate(1, 0, 0, 1, (512,))
            psend(cref(1, 0, 0, 2), pfull.at[0], 2, "P+")
        elif dp == 3:
            arrived(popp.at[1], p_send.at[0], p_recv.at[1])
            fetch([(popp.at[1], RB.at[pl.ds(512, 128)])])
            accumulate(3, 0, 1, 1, (512,))
            psend(cref(3, 0, 0, 2), pfull.at[1], 3, "P-")
        else:
            arrived(pfull.at[0], p_send.at[0], p_recv.at[2])
            arrived(pfull.at[1], p_send.at[0], p_recv.at[3])
            fetch([(pfull.at[0], RB.at[pl.ds(0, 256)]), (pfull.at[1], RB.at[pl.ds(256, 256)])])
            accumulate(0, 0, 0, 2, (0, 256))
            for k, out in enumerate((mixed, gtok)):
                cp = pltpu.make_async_copy(cref(0, 0, k), out, loc.at[11 + k])
                cp.start()
                outs.append(cp)

    T0, T1, T2 = (0, 7), (7, 5), (12, 4)
    take(3, 0, 0)
    push(3, 0, 0, "P+")
    take(1, 0, 1)
    push(1, 0, 1, "P-")
    take(0, 3, 0)
    push(0, 3, 0, "Q+")
    take(0, 1, 1)
    push(0, 1, 1, "Q-")
    push(3, 0, 0, "Q+")
    push(1, 0, 1, "Q-")
    take(1, 0, 0)
    push(1, 0, 0, "Q+")
    take(3, 0, 1)
    push(3, 0, 1, "Q-")
    take(0, 1, 0)
    take(0, 3, 1)
    for chip in ((1, 0), (3, 0), (0, 1), (0, 3)):
        for k in range(2):
            push_sib(*chip, k)
    w_fwd(0)
    w_own(1, (1, 2))
    picks([(0, 0)], L)
    for k in range(2):
        take(2, 0, k)
    push(2, 0, 0, "Q+")
    push(2, 0, 1, "Q-")
    push(2, 0, 0, "Q-")
    push(2, 0, 1, "Q+")
    for k in range(2):
        push_sib(2, 0, k)
        take(0, 2, k)
        push_sib(0, 2, k)
    picks([(0, 1), (0, 3), (1, 0), (3, 0)], L)
    for dp in (3, 1):
        take(dp, 3, 0)
        push(dp, 3, 0, "Q+")
        take(dp, 1, 1)
        push(dp, 1, 1, "Q-")
    for dp in (3, 1):
        push_sib(dp, 3, 0)
        push_sib(dp, 1, 1)
    picks([(0, 2), (2, 0)], L)
    take(2, 3, 0)
    push(2, 3, 0, "Q+")
    take(2, 1, 1)
    push(2, 1, 1, "Q-")
    for dp in (3, 1):
        push(dp, 0, 0, "Q-")
        push(dp, 0, 1, "Q+")
    take(2, 1, 0)
    take(2, 3, 1)
    for chip in ((2, 1), (2, 3)):
        for k in range(2):
            push_sib(*chip, k)
    w_last(0)
    for cp in own_w:
        cp.wait()
    forward(0, T0)
    outputs(0, T0)
    for dp in (3, 1):
        for k in range(2):
            take(dp, 2, k)
            push_sib(dp, 2, k)
    w_fwd(1)
    picks([(2, 1), (2, 3), (1, 2), (3, 2)], L)
    for k in range(2):
        take(2, 2, k)
        push_sib(2, 2, k)
    picks([(2, 2)], L)
    forward(0, T1)
    outputs(0, T1)
    w_last(1)
    forward(1, T1)
    outputs(1, T1)
    yd_sends([(2, 2), (1, 2), (3, 2), (2, 1), (2, 3)])
    forward(1, T0)
    outputs(1, T0)
    yd_sends([(0, 2), (0, 1), (0, 3), (2, 0), (1, 0), (3, 0), (0, 0)])
    yd_start(0)
    for dp, dq in far:
        combine(dp, dq)
        q_first(dp)
    combine(2, 1)
    combine(2, 3)
    for dp in (3, 1):
        take(dp, 1, 0)
        push_sib(dp, 1, 0)
        take(dp, 3, 1)
        push_sib(dp, 3, 1)
    picks([(1, 1), (1, 3), (3, 1), (3, 3)], RB)
    q_second(2)
    forward(0, T2)
    outputs(0, T2)
    for cp in flying["Z"]:
        cp.wait_send()
    flying["Z"] = []
    weight_grads(0)
    combine(0, 1)
    combine(0, 3, False)
    forward(1, T2)
    outputs(1, T2)
    yd_sends([(1, 1), (1, 3), (3, 1), (3, 3)])
    yd_start(8)
    q_second(0)
    weight_grads(1)
    combine(1, 1)
    combine(1, 3)
    q_second(1)
    z_second(0)
    combine(3, 1)
    combine(3, 3)
    q_second(3)
    z_second(1)
    for dp, dq in mine:
        combine(dp, dq)
    q_third(2)
    q_third(1)
    q_third(3)
    z_third(0)
    q_third(0)
    z_third(1)
    for cp in outs:
        cp.wait()
    for line in flying.values():
        for cp in line:
            cp.wait_send()


def per_device(tokens, expert_ids, gate_prob, w_gate, w_up, w_down, grad_out):
    sds = jax.ShapeDtypeStruct
    hbm = pl.BlockSpec(memory_space=pl.ANY)
    dma = pltpu.SemaphoreType.DMA
    out_shape = (
        sds((TOK, D), BF),
        sds((TOK, D), BF),
        sds((2, 512, FF), BF),
        sds((2, 512, FF), BF),
        sds((2, FF, 512), BF),
        sds((16, 256, XW), BF),
        sds((16, 256, D), BF),
        sds((16, 96, 2 * D), BF),
        sds((4, 2, TOK, D), BF),
        sds((4, 2, 256, D), BF),
        sds((2, TOK, D), BF),
        sds((2, 256, D), BF),
    )
    scratch = [
        pltpu.VMEM((4 * ROWS, D), BF),
        pltpu.VMEM((1024, D), BF),
        pltpu.VMEM((2, D, 2 * FF), BF),
        pltpu.VMEM((2, 4, FF, 512), BF),
        pltpu.VMEM((16, 96, 2 * D), BF),
        pltpu.VMEM((2, ROWS, FF), BF),
        pltpu.VMEM((2, ROWS, 2 * FF), BF),
        pltpu.VMEM((2 * ROWS, 128), F32),
        pltpu.VMEM((16, 192, TOK), BF),
        pltpu.VMEM((2, 2, 32, 128), BF),
        pltpu.VMEM((128, 128), BF),
        pltpu.VMEM((2, 96, 2 * D), BF),
        pltpu.VMEM((1024, D), BF),
        pltpu.VMEM((2, 2, 256, 2 * FF), BF),
        pltpu.VMEM((2, 2, 512, 2 * FF), BF),
        pltpu.VMEM((2, 2, 192, 512), BF),
        pltpu.VMEM((2, 2, FF, 512), BF),
        pltpu.VMEM((1024, D), BF),
        dma((30,)), dma((32,)), dma((32,)), dma((32,)),
        dma((20,)), dma((20,)), dma((16,)), dma((16,)),
        dma((16,)), dma((16,)), dma((4,)), dma((4,)),
        dma((16,)), dma((16,)), dma((13,)), dma((2, 6)), dma((2,)), dma((5,)),
    ]
    res = pl.pallas_call(
        kernel,
        out_shape=out_shape,
        in_specs=[hbm] * 5 + [pl.BlockSpec(memory_space=pltpu.VMEM)] * 2,
        out_specs=[hbm] * len(out_shape),
        scratch_shapes=scratch,
        compiler_params=pltpu.CompilerParams(
            collective_id=0, has_side_effects=True, vmem_limit_bytes=63 * 1024 * 1024
        ),
    )(tokens, grad_out, w_gate, w_up, w_down, expert_ids, gate_prob)
    return res[:5]


def solution(mesh):
    return jax.shard_map(
        per_device,
        mesh=mesh,
        in_specs=(
            P(("expert", "dp"), None),
            P(("expert", "dp"), None),
            P(("expert", "dp"), None),
            P("expert", "dp", None),
            P("expert", "dp", None),
            P("expert", None, "dp"),
            P(("expert", "dp"), None),
        ),
        out_specs=(
            P(("expert", "dp"), None),
            P(("expert", "dp"), None),
            P("expert", "dp", None),
            P("expert", "dp", None),
            P("expert", None, "dp"),
        ),
        check_vma=False,
    )
```

```python
import jax
import jax.numpy as jnp
from jax import lax
from jax.experimental import pallas as pl
from jax.experimental.pallas import tpu as pltpu
from jax.sharding import PartitionSpec as P

MESH = pl.DeviceIdType.MESH
BF = jnp.bfloat16
F32 = jnp.float32
D = 2048
FF = 384
TOK = 128
CAP = 24
KEEP = {"S": 6, "P": 6, "Q": 12, "Z": 8}
ROWS = 768
XW = D + 128
PLACES = [
    (0, 0), (0, 1), (0, 3), (1, 0), (3, 0), (0, 2), (2, 0),
    (2, 1), (2, 3), (1, 2), (3, 2), (2, 2),
    (1, 1), (1, 3), (3, 1), (3, 3),
]
NT = (((1,), (1,)), ((), ()))
TN = (((0,), (0,)), ((), ()))
NN = (((1,), (0,)), ((), ()))


def dot(a, b, dims):
    return lax.dot_general(a, b, dims, preferred_element_type=F32)


def kernel(
    tok, g, wgate, wup, wdown, eids, gprob,
    own_r, own_gu, own_d, zfg, zfd, pfull,
    xbuf, gbuf, ysib, qopp, qfull, popp,
    S, L, Wgu, Wd, YD, H, DAB, PW, P4, MB, MT, YL, RB, zhg, zhd, early,
    a_send, a_recv, s_send, s_recv, w_send, w_recv, y_send, y_recv,
    q_send, q_recv, p_send, p_recv, z_send, z_recv, loc, ld, yl_sem, m_send,
):
    me = lax.axis_index("expert")
    z = lax.axis_index("dp")
    c = lax.rem(me, 2)
    x = lax.rem(me // 2, 4)
    y = me // 8
    sib = {"expert": me + 1 - 2 * c}
    zr, zl, zo = lax.rem(z + 1, 4), lax.rem(z + 3, 4), lax.rem(z + 2, 4)

    def pq(dp, dq):
        dx = dp + c * (dq - dp)
        dy = dq + c * (dp - dq)
        return {"expert": (lax.rem(y + dy, 4) * 4 + lax.rem(x + dx, 4)) * 2 + c}

    dev = {"P+": pq(1, 0), "P-": pq(3, 0), "Q+": pq(0, 1), "Q-": pq(0, 3), "S": sib, "Z+": {"dp": zr}, "Z-": {"dp": zl}}

    def slot(dp, dq):
        k0, k1 = PLACES.index((dp, dq)), PLACES.index((dq, dp))
        return k0 + c * (k1 - k0)

    barrier = pltpu.get_barrier_semaphore()
    for d in dev.values():
        pl.semaphore_signal(barrier, inc=1, device_id=d, device_id_type=MESH)

    flying = {}

    def send(src, dst, ssem, rsem, to):
        cp = pltpu.make_async_remote_copy(
            src_ref=src, dst_ref=dst, send_sem=ssem, recv_sem=rsem, device_id=dev[to], device_id_type=MESH
        )
        line = flying.setdefault(to[0], [])
        while len(line) >= KEEP[to[0]]:
            line.pop(0).wait_send()
        cp.start()
        line.append(cp)

    def arrived(dst, ssem, rsem):
        pltpu.make_async_remote_copy(
            src_ref=dst, dst_ref=dst, send_sem=ssem, recv_sem=rsem, device_id=dev["S"], device_id_type=MESH
        ).wait_recv()

    half = pl.ds(pl.multiple_of(c * TOK, TOK), TOK)
    other = pl.ds(pl.multiple_of((1 - c) * TOK, TOK), TOK)
    bufs = (xbuf, gbuf)
    counts = {"a": 0, "m": 0}

    def nxt(name):
        counts[name] += 1
        return counts[name] - 1

    def aidx(dp, dq, k):
        return (dp * 4 + dq) * 2 + k

    def blk(dp, dq, k):
        return bufs[k].at[slot(dp, dq), half, :]

    def push(dp, dq, k, to):
        ddp, ddq = dp, dq
        if to == "P+":
            ddp = (dp + 3) % 4
        elif to == "P-":
            ddp = (dp + 1) % 4
        elif to == "Q+":
            ddq = (dq + 3) % 4
        elif to == "Q-":
            ddq = (dq + 1) % 4
        launch(dp, dq, k, slot(ddp, ddq), a_send, nxt("a"), a_recv.at[aidx(ddp, ddq, k)], to)

    def launch(dp, dq, k, r, ssem, i, rsem, to):
        dst = bufs[k].at[r, half, :]
        if dp or dq:
            send(blk(dp, dq, k), dst, ssem.at[i], rsem, to)
        elif k == 1:
            send(g, dst, ssem.at[i], rsem, to)
        else:
            send(tok, bufs[0].at[r, half, pl.ds(0, D)], ssem.at[i], rsem, to)
            send(MT, bufs[0].at[r, half, pl.ds(D, 128)], m_send.at[counts["m"]], rsem, to)
            counts["m"] += 1

    def push_sib(dp, dq, k):
        i = aidx(dp, dq, k)
        launch(dp, dq, k, slot(dp, dq), s_send, i, s_recv.at[i], "S")

    def take(dp, dq, k):
        i = aidx(dp, dq, k)
        arrived(bufs[k].at[slot(dp, dq), half, :], a_send.at[0], a_recv.at[i])

    def take_sib(dp, dq, k):
        i = aidx(dq, dp, k)
        arrived(bufs[k].at[slot(dp, dq), other, :], s_send.at[0], s_recv.at[i])

    prob_in = gprob[...]
    hi = prob_in.astype(BF)
    mid = (prob_in - hi.astype(F32)).astype(BF)
    low = (prob_in - hi.astype(F32) - mid.astype(F32)).astype(BF)
    meta = [eids[...].astype(F32), hi.astype(F32), mid.astype(F32), low.astype(F32), jnp.zeros((96, TOK), F32)]
    MT[...] = jnp.concatenate(meta, axis=0).astype(BF)
    pl.semaphore_wait(barrier, 7)

    def zrows(i):
        return pl.ds(pl.multiple_of(i * 512, 512), 512)

    wsrc = (wgate, wup, wdown)

    def wdst(e, k, i):
        if k == 2:
            return Wd.at[e, i]
        return Wgu.at[e, zrows(i), pl.ds(k * FF, FF)]

    own_w = [
        pltpu.make_async_copy(wsrc[k].at[e], wdst(e, k, z), loc.at[5 + 3 * e + k]) for e in range(2) for k in range(3)
    ]

    def w_own(e, kinds=(0, 1, 2)):
        for k in kinds:
            for j, to in enumerate(("Z+", "Z-")):
                wsend(wsrc[k].at[e], wdst(e, k, z), e * 10 + 3 * j + k, to)

    def wsend(src, dst, i, to):
        send(src, dst, w_send.at[i], w_recv.at[i], to)

    def w_parts(e, i):
        lo = pl.ds(pl.multiple_of(i * 512, 512), 256)
        hi = pl.ds(pl.multiple_of(i * 512 + 256, 256), 256)
        return (Wgu.at[e, lo], Wgu.at[e, hi], Wd.at[e, i, pl.ds(0, 192)], Wd.at[e, i, pl.ds(192, 192)])

    def w_fwd(e):
        for k in range(3):
            arrived(wdst(e, k, zl), w_send.at[0], w_recv.at[e * 10 + k])
            arrived(wdst(e, k, zr), w_send.at[0], w_recv.at[e * 10 + 3 + k])
        for j in range(4):
            part = w_parts(e, (zl, zr)[j % 2])[j]
            wsend(part, part, e * 10 + 6 + j, ("Z+", "Z-")[j % 2])

    def w_last(e):
        for j in range(4):
            arrived(w_parts(e, zo)[j], w_send.at[0], w_recv.at[e * 10 + 6 + j])

    for k in range(2):
        push(0, 0, k, "P+")
        push(0, 0, 1 - k, "P-")
        push(0, 0, k, "Q+")
        push(0, 0, 1 - k, "Q-")
        if k == 0:
            w_own(0)
            w_own(1, (0,))
    push_sib(0, 0, 0)
    push_sib(0, 0, 1)
    for cp in own_w:
        cp.start()

    tri = (
        lax.broadcasted_iota(jnp.int32, (TOK, TOK), 0) <= lax.broadcasted_iota(jnp.int32, (TOK, TOK), 1)
    ).astype(F32).astype(BF)
    row8 = lax.broadcasted_iota(jnp.int32, (8, TOK), 0)
    slot_row = lax.broadcasted_iota(jnp.int32, (2 * CAP, TOK), 0).astype(F32)
    cf = c.astype(F32)
    e_own = (2 * me).astype(F32)
    e_sib = (2 * (me + 1 - 2 * c)).astype(F32)

    def load(chip, b, buf):
        r = 0 if chip == (0, 0) else slot(*chip)
        for cp in load_copies(r, b, buf):
            cp.start()

    def load_copies(r, b, buf):
        if isinstance(r, int):
            r0 = b * 512
            mine, theirs = pl.ds(pl.multiple_of(r0 + c * TOK, TOK), TOK), pl.ds(pl.multiple_of(r0 + TOK - c * TOK, TOK), TOK)
            mine_g = pl.ds(pl.multiple_of(r0 + 256 + c * TOK, TOK), TOK)
            theirs_g = pl.ds(pl.multiple_of(r0 + 256 + TOK - c * TOK, TOK), TOK)
            few = pl.ds(pl.multiple_of((1 - c) * TOK, TOK), 32)
            return (
                pltpu.make_async_copy(tok, buf.at[mine, :], ld.at[b, 0]),
                pltpu.make_async_copy(xbuf.at[0, other, pl.ds(0, D)], buf.at[theirs, :], ld.at[b, 1]),
                pltpu.make_async_copy(g, buf.at[mine_g, :], ld.at[b, 2]),
                pltpu.make_async_copy(gbuf.at[0, other, :], buf.at[theirs_g, :], ld.at[b, 3]),
                pltpu.make_async_copy(MT.at[pl.ds(0, 32), :], MB.at[b, c], ld.at[b, 4]),
                pltpu.make_async_copy(xbuf.at[0, few, pl.ds(D, 128)], MB.at[b, 1 - c], ld.at[b, 5]),
            )
        return (
            pltpu.make_async_copy(xbuf.at[r, :, pl.ds(0, D)], buf.at[pl.ds(b * 512, 256), :], ld.at[b, 0]),
            pltpu.make_async_copy(gbuf.at[r], buf.at[pl.ds(b * 512 + 256, 256), :], ld.at[b, 1]),
            pltpu.make_async_copy(xbuf.at[r, pl.ds(0, 32), pl.ds(D, 128)], MB.at[b, 0], ld.at[b, 2]),
            pltpu.make_async_copy(xbuf.at[r, pl.ds(TOK, 32), pl.ds(D, 128)], MB.at[b, 1], ld.at[b, 3]),
        )

    def pick(chip, b, buf):
        r = 0 if chip == (0, 0) else slot(*chip)
        for cp in load_copies(r, b, buf):
            cp.wait()
        ids, prob = [], []
        for t in range(2):
            ids.append(MB[b, t, 0:8].astype(F32))
            prob.append(
                MB[b, t, 8:16].astype(F32) + (MB[b, t, 16:24].astype(F32) + MB[b, t, 24:32].astype(F32))
            )
        ids_c = jnp.where(c == 0, ids[0], ids[1])
        todo = [(ids[0], e_own), (ids[1], e_own), (ids[0], e_own + 1), (ids[1], e_own + 1), (ids_c, e_sib), (ids_c, e_sib + 1)]
        hit = jnp.zeros((8, TOK), F32)
        pv = []
        for j, (idv, e) in enumerate(todo):
            m = jnp.where(idv == e, 1.0, 0.0)
            if j < 4:
                pv.append(jnp.sum(m * prob[j % 2], axis=0, keepdims=True))
            hit = jnp.where(row8 == j, jnp.sum(m, axis=0, keepdims=True), hit)
        rank = dot(hit.astype(BF), tri, NN)
        key = jnp.where(hit > 0.5, rank - 1.0, -1000.0)
        p256, pown, psib = [], [], []
        for e in range(2):
            p0 = jnp.where(key[2 * e : 2 * e + 1] == slot_row, 1.0, 0.0)
            p1 = jnp.where(key[2 * e + 1 : 2 * e + 2] + CAP == slot_row, 1.0, 0.0)
            w = jnp.sum(p0 * pv[2 * e] + p1 * pv[2 * e + 1], axis=1, keepdims=True)
            at = pl.ds(pl.multiple_of(e * ROWS + r * 48, 16), 48)
            PW[at, :] = jnp.broadcast_to(w, (48, 128))
            p256.append(jnp.concatenate([p0, p1], axis=1))
            pown.append(jnp.where(c == 0, p0, p1))
            psib.append(jnp.where(key[4 + e : 5 + e] + CAP * cf == slot_row, 1.0, 0.0))
        P4[r] = jnp.concatenate(pown + psib, axis=0).astype(BF)
        pick_m = jnp.concatenate(p256, axis=0).astype(BF)

        def cols(n, _):
            cc = pl.ds(pl.multiple_of(n * 1024, 1024), 1024)
            for t in range(2):
                src = buf[pl.ds(b * 512 + t * 256, 256), cc]
                got = dot(pick_m, src, NN).astype(BF)
                for e in range(2):
                    at = pl.ds(pl.multiple_of(t * 2 * ROWS + e * ROWS + r * 48, 16), 48)
                    S[at, cc] = got[e * 48 : e * 48 + 48]
            return 0

        lax.fori_loop(0, 2, cols, 0)

    def picks(some, buf):
        for i, chip in enumerate(some):
            for j in (i, i + 1):
                if j < len(some) and (j > i or i == 0):
                    for k in range(2):
                        take_sib(*some[j], k)
                    load(some[j], j % 2, buf)
            pick(chip, i % 2, buf)

    def forward(e, tile):
        first, n = tile
        lo, cnt = first * 48, n * 48
        xs = S[e * ROWS + lo : e * ROWS + lo + cnt, :]
        ab = dot(xs, Wgu[e], NN)
        g0 = (2 + e) * ROWS + lo
        dh = dot(S[g0 : g0 + cnt, 0:512], Wd[e, 0], NT)
        for i in range(1, 4):
            dh = dh + dot(S[g0 : g0 + cnt, i * 512 : i * 512 + 512], Wd[e, i], NT)
        w = PW[e * ROWS + lo : e * ROWS + lo + cnt, 0:1]
        a, b = ab[:, :FF], ab[:, FF:]
        s = 1.0 / (1.0 + jnp.exp(-a))
        act = a * s
        dh = dh * w
        H[e, lo : lo + cnt, :] = (act * b * w).astype(BF)
        DAB[e, lo : lo + cnt, 0:FF] = (dh * b * s * (1.0 + a * (1.0 - s))).astype(BF)
        DAB[e, lo : lo + cnt, FF:] = (dh * act).astype(BF)

    def outputs(e, tile):
        first, n = tile
        lo, cnt = first * 48, n * 48
        for i in range(4):
            yv = dot(H[e, lo : lo + cnt, :], Wd[e, i], NN).astype(BF)
            YD[first : first + n, e * 48 : e * 48 + 48, i * 512 : i * 512 + 512] = yv.reshape(n, 48, 512)
        for i in range(4):
            dv = dot(DAB[e, lo : lo + cnt, :], Wgu[e, i * 512 : i * 512 + 512, :], NT).astype(BF)
            YD[first : first + n, e * 48 : e * 48 + 48, D + i * 512 : D + i * 512 + 512] = dv.reshape(n, 48, 512)

    def weight_grads(e):
        def part(j, _):
            i = lax.rem(z + j, 4)
            cc = zrows(i)
            xs = S[e * ROWS : e * ROWS + ROWS, cc]
            gs = S[(2 + e) * ROWS : (3 + e) * ROWS, cc]
            Wgu[e, cc, :] = dot(xs, DAB[e], TN).astype(BF)
            Wd[e, i] = dot(H[e], gs, TN).astype(BF)
            return 0

        lax.fori_loop(2, 3, part, 0)
        z_first(e)
        lax.fori_loop(3, 6, part, 0)

    def zsend(src, dst, i, to):
        send(src, dst, z_send.at[i], z_recv.at[i], to)

    def z_first(e):
        base = e * 8
        lo = pl.ds(pl.multiple_of(zo * 512, 512), 256)
        hi = pl.ds(pl.multiple_of(zo * 512 + 256, 256), 256)
        zsend(Wgu.at[e, lo], zhg.at[e, 0], base + 0, "Z+")
        zsend(Wgu.at[e, hi], zhg.at[e, 1], base + 1, "Z-")
        zsend(Wd.at[e, zo, pl.ds(0, 192)], zhd.at[e, 0], base + 2, "Z+")
        zsend(Wd.at[e, zo, pl.ds(192, 192)], zhd.at[e, 1], base + 3, "Z-")

    def z_second(e):
        base = e * 8
        for i, (dst, rows) in enumerate(((zhg.at[e, 0], 0), (zhg.at[e, 1], 0), (zhd.at[e, 0], 0), (zhd.at[e, 1], 0))):
            arrived(dst, z_send.at[0], z_recv.at[base + i])

        def add(j, _):
            for i, (zz, off) in enumerate(((zr, 0), (zl, 256))):
                at = pl.ds(pl.multiple_of(zz * 512 + off + j * 32, 32), 32)
                Wgu[e, at, :] = (Wgu[e, at, :].astype(F32) + zhg[e, i, pl.ds(j * 32, 32), :].astype(F32)).astype(BF)
            return 0

        lax.fori_loop(0, 8, add, 0)

        def add_d(j, _):
            for i, (zz, off) in enumerate(((zr, 0), (zl, 192))):
                at = pl.ds(pl.multiple_of(off + j * 32, 32), 32)
                Wd[e, zz, at, :] = (Wd[e, zz, at, :].astype(F32) + zhd[e, i, pl.ds(j * 32, 32), :].astype(F32)).astype(BF)
            return 0

        lax.fori_loop(0, 6, add_d, 0)
        zsend(Wgu.at[e, zrows(zr)], zfg.at[e, 0], base + 4, "Z+")
        zsend(Wgu.at[e, zrows(zl)], zfg.at[e, 1], base + 5, "Z-")
        zsend(Wd.at[e, zr], zfd.at[e, 0], base + 6, "Z+")
        zsend(Wd.at[e, zl], zfd.at[e, 1], base + 7, "Z-")

    outs = []

    def z_third(e):
        base = e * 8
        for i, dst in enumerate((zfg.at[e, 0], zfg.at[e, 1], zfd.at[e, 0], zfd.at[e, 1])):
            arrived(dst, z_send.at[0], z_recv.at[base + 4 + i])

    def z_own(e):
        for i, (src, dst) in enumerate(((Wgu.at[e, zrows(z)], own_gu.at[e]), (Wd.at[e, z], own_d.at[e]))):
            cp = pltpu.make_async_copy(src, dst, loc.at[e * 2 + i])
            cp.start()
            outs.append(cp)

    far = [(2, 2), (1, 2), (3, 2), (0, 2)]
    near = [(2, 1), (2, 3), (0, 1), (0, 3), (1, 1), (1, 3), (3, 1), (3, 3)]
    mine = [(2, 0), (1, 0), (3, 0), (0, 0)]
    chips = far + near + mine

    def yd_sends(some):
        for i, (dp, dq) in enumerate(chips):
            if (dp, dq) in some:
                r = slot(dq, dp)
                send(YD.at[r], ysib.at[r], y_send.at[i], y_recv.at[i], "S")

    def yd_load(i):
        r = slot(*chips[i])
        return pltpu.make_async_copy(ysib.at[r], YL.at[i % 2], yl_sem.at[i % 2])

    def yd_start(i):
        r = slot(*chips[i])
        arrived(ysib.at[r], y_send.at[0], y_recv.at[i])
        yd_load(i).start()

    def cblk(dp, dq, k=0, n=1):
        if dq == 2:
            return L, dp * 256 + k * 128, n * 128
        if dp in (0, 2) and dq:
            return early, dp * 256 + dq // 2 * 256 + k * 128, n * 128
        return S, dp * 768 + {0: 0, 1: 256, 3: 512}[dq] + k * 128, n * 128

    def cref(dp, dq, k=0, n=1):
        ref, row, cnt = cblk(dp, dq, k, n)
        return ref.at[pl.ds(row, cnt), :]

    def combine(dp, dq, ahead=True):
        i = chips.index((dp, dq))
        if i + 1 < 16 and ahead:
            yd_start(i + 1)
        yd_load(i).wait()
        r = slot(dp, dq)
        ref, row, _ = cblk(dp, dq)
        pm = P4[r]

        def cols(n, _):
            cc = pl.ds(pl.multiple_of(n * 512, 512), 512)
            for k in range(2):
                ck = pl.ds(pl.multiple_of(k * D + n * 512, 512), 512)
                rows = jnp.concatenate([YD[r, :, ck], YL[i % 2, :, ck]], axis=0)
                ref[row + k * 128 : row + k * 128 + 128, cc] = dot(pm, rows, TN).astype(BF)
            return 0

        lax.fori_loop(0, 4, cols, 0)

    def fetch(pairs):
        cps = [pltpu.make_async_copy(s, d, ld.at[0, i]) for i, (s, d) in enumerate(pairs)]
        for cp in cps:
            cp.start()
        for cp in cps:
            cp.wait()

    def accumulate(dp, dq, k, n, parts):
        ref, row, cnt = cblk(dp, dq, k, n)

        def add(j, _):
            at = pl.ds(pl.multiple_of(row + j * 16, 16), 16)
            total = ref[at, :].astype(F32)
            for off in parts:
                total = total + RB[pl.ds(pl.multiple_of(off + j * 16, 16), 16), :].astype(F32)
            ref[at, :] = total.astype(BF)
            return 0

        lax.fori_loop(0, cnt // 16, add, 0)

    def qsend(src, dst, dp, j, to):
        send(src, dst, q_send.at[dp * 4 + j], q_recv.at[dp * 4 + j], to)

    def q_first(dp):
        qsend(cref(dp, 2, 0), qopp.at[dp, 0], dp, 0, "Q+")
        qsend(cref(dp, 2, 1), qopp.at[dp, 1], dp, 1, "Q-")

    def q_second(dp):
        arrived(qopp.at[dp, 0], q_send.at[0], q_recv.at[dp * 4 + 0])
        arrived(qopp.at[dp, 1], q_send.at[0], q_recv.at[dp * 4 + 1])
        fetch([(qopp.at[dp, 0], RB.at[pl.ds(512, 128)]), (qopp.at[dp, 1], RB.at[pl.ds(640, 128)])])
        accumulate(dp, 1, 0, 1, (512,))
        qsend(cref(dp, 1, 0, 2), qfull.at[dp, 0], dp, 2, "Q+")
        accumulate(dp, 3, 1, 1, (640,))
        qsend(cref(dp, 3, 0, 2), qfull.at[dp, 1], dp, 3, "Q-")

    def psend(src, dst, j, to):
        send(src, dst, p_send.at[j], p_recv.at[j], to)

    def q_third(dp):
        arrived(qfull.at[dp, 0], q_send.at[0], q_recv.at[dp * 4 + 2])
        arrived(qfull.at[dp, 1], q_send.at[0], q_recv.at[dp * 4 + 3])
        fetch([(qfull.at[dp, 0], RB.at[pl.ds(0, 256)]), (qfull.at[dp, 1], RB.at[pl.ds(256, 256)])])
        accumulate(dp, 0, 0, 2, (0, 256))
        if dp == 2:
            psend(cref(2, 0, 0), popp.at[0], 0, "P+")
            psend(cref(2, 0, 1), popp.at[1], 1, "P-")
        elif dp == 1:
            arrived(popp.at[0], p_send.at[0], p_recv.at[0])
            fetch([(popp.at[0], RB.at[pl.ds(512, 128)])])
            accumulate(1, 0, 0, 1, (512,))
            psend(cref(1, 0, 0, 2), pfull.at[0], 2, "P+")
        elif dp == 3:
            arrived(popp.at[1], p_send.at[0], p_recv.at[1])
            fetch([(popp.at[1], RB.at[pl.ds(512, 128)])])
            accumulate(3, 0, 1, 1, (512,))
            psend(cref(3, 0, 0, 2), pfull.at[1], 3, "P-")
        else:
            cp = pltpu.make_async_copy(cref(0, 0, 0, 2), own_r, loc.at[4])
            cp.start()
            outs.append(cp)
            arrived(pfull.at[0], p_send.at[0], p_recv.at[2])
            arrived(pfull.at[1], p_send.at[0], p_recv.at[3])

    T0, T1, T2 = (0, 7), (7, 5), (12, 4)
    take(3, 0, 0)
    push(3, 0, 0, "P+")
    take(1, 0, 1)
    push(1, 0, 1, "P-")
    take(0, 3, 0)
    push(0, 3, 0, "Q+")
    take(0, 1, 1)
    push(0, 1, 1, "Q-")
    push(3, 0, 0, "Q+")
    push(1, 0, 1, "Q-")
    take(1, 0, 0)
    push(1, 0, 0, "Q+")
    take(3, 0, 1)
    push(3, 0, 1, "Q-")
    take(0, 1, 0)
    take(0, 3, 1)
    for chip in ((1, 0), (3, 0), (0, 1), (0, 3)):
        for k in range(2):
            push_sib(*chip, k)
    w_fwd(0)
    w_own(1, (1, 2))
    picks([(0, 0)], L)
    for k in range(2):
        take(2, 0, k)
    push(2, 0, 0, "Q+")
    push(2, 0, 1, "Q-")
    push(2, 0, 0, "Q-")
    push(2, 0, 1, "Q+")
    for k in range(2):
        push_sib(2, 0, k)
        take(0, 2, k)
        push_sib(0, 2, k)
    picks([(0, 1), (0, 3), (1, 0), (3, 0)], L)
    for dp in (3, 1):
        take(dp, 3, 0)
        push(dp, 3, 0, "Q+")
        take(dp, 1, 1)
        push(dp, 1, 1, "Q-")
    for dp in (3, 1):
        push_sib(dp, 3, 0)
        push_sib(dp, 1, 1)
    picks([(0, 2), (2, 0)], L)
    take(2, 3, 0)
    push(2, 3, 0, "Q+")
    take(2, 1, 1)
    push(2, 1, 1, "Q-")
    for dp in (3, 1):
        push(dp, 0, 0, "Q-")
        push(dp, 0, 1, "Q+")
    take(2, 1, 0)
    take(2, 3, 1)
    for chip in ((2, 1), (2, 3)):
        for k in range(2):
            push_sib(*chip, k)
    w_last(0)
    for cp in own_w:
        cp.wait()
    forward(0, T0)
    outputs(0, T0)
    for dp in (3, 1):
        for k in range(2):
            take(dp, 2, k)
            push_sib(dp, 2, k)
    w_fwd(1)
    picks([(2, 1), (2, 3), (1, 2), (3, 2)], L)
    for k in range(2):
        take(2, 2, k)
        push_sib(2, 2, k)
    picks([(2, 2)], L)
    forward(0, T1)
    outputs(0, T1)
    w_last(1)
    forward(1, T1)
    outputs(1, T1)
    yd_sends([(2, 2), (1, 2), (3, 2), (2, 1), (2, 3)])
    forward(1, T0)
    outputs(1, T0)
    yd_sends([(0, 2), (0, 1), (0, 3), (2, 0), (1, 0), (3, 0), (0, 0)])
    yd_start(0)
    for dp, dq in far:
        combine(dp, dq)
        q_first(dp)
    combine(2, 1)
    combine(2, 3)
    for dp in (3, 1):
        take(dp, 1, 0)
        push_sib(dp, 1, 0)
        take(dp, 3, 1)
        push_sib(dp, 3, 1)
    picks([(1, 1), (1, 3), (3, 1), (3, 3)], RB)
    q_second(2)
    forward(0, T2)
    outputs(0, T2)
    for cp in flying["Z"]:
        cp.wait_send()
    flying["Z"] = []
    weight_grads(0)
    combine(0, 1)
    combine(0, 3, False)
    forward(1, T2)
    outputs(1, T2)
    yd_sends([(1, 1), (1, 3), (3, 1), (3, 3)])
    yd_start(8)
    q_second(0)
    weight_grads(1)
    z_own(0)
    z_own(1)
    combine(1, 1)
    combine(1, 3)
    q_second(1)
    z_second(0)
    combine(3, 1)
    combine(3, 3)
    q_second(3)
    z_second(1)
    for dp, dq in mine:
        combine(dp, dq)
    q_third(2)
    q_third(1)
    q_third(3)
    z_third(0)
    q_third(0)
    z_third(1)
    for cp in outs:
        cp.wait()
    for line in flying.values():
        for cp in line:
            cp.wait_send()


def finish(own_r, own_gu, own_d, zfg, zfd, pfull, mixed, gtok, ggate, gup, gdown):
    for k, out in enumerate((mixed, gtok)):
        out[...] = (own_r[k].astype(F32) + pfull[0, k].astype(F32) + pfull[1, k].astype(F32)).astype(BF)
    for e in range(2):
        gu = (own_gu[e].astype(F32) + zfg[e, 0].astype(F32) + zfg[e, 1].astype(F32)).astype(BF)
        ggate[e] = gu[:, :FF]
        gup[e] = gu[:, FF:]
        gdown[e] = (own_d[e].astype(F32) + zfd[e, 0].astype(F32) + zfd[e, 1].astype(F32)).astype(BF)


def per_device(tokens, expert_ids, gate_prob, w_gate, w_up, w_down, grad_out):
    sds = jax.ShapeDtypeStruct
    hbm = pl.BlockSpec(memory_space=pl.ANY)
    dma = pltpu.SemaphoreType.DMA
    out_shape = (
        sds((256, D), BF),
        sds((2, 512, 2 * FF), BF),
        sds((2, FF, 512), BF),
        sds((2, 2, 512, 2 * FF), BF),
        sds((2, 2, FF, 512), BF),
        sds((2, 256, D), BF),
        sds((16, 256, XW), BF),
        sds((16, 256, D), BF),
        sds((16, 96, 2 * D), BF),
        sds((4, 2, TOK, D), BF),
        sds((4, 2, 256, D), BF),
        sds((2, TOK, D), BF),
    )
    scratch = [
        pltpu.VMEM((4 * ROWS, D), BF),
        pltpu.VMEM((1024, D), BF),
        pltpu.VMEM((2, D, 2 * FF), BF),
        pltpu.VMEM((2, 4, FF, 512), BF),
        pltpu.VMEM((16, 96, 2 * D), BF),
        pltpu.VMEM((2, ROWS, FF), BF),
        pltpu.VMEM((2, ROWS, 2 * FF), BF),
        pltpu.VMEM((2 * ROWS, 128), F32),
        pltpu.VMEM((16, 192, TOK), BF),
        pltpu.VMEM((2, 2, 32, 128), BF),
        pltpu.VMEM((128, 128), BF),
        pltpu.VMEM((2, 96, 2 * D), BF),
        pltpu.VMEM((1024, D), BF),
        pltpu.VMEM((2, 2, 256, 2 * FF), BF),
        pltpu.VMEM((2, 2, 192, 512), BF),
        pltpu.VMEM((1024, D), BF),
        dma((30,)), dma((32,)), dma((32,)), dma((32,)),
        dma((20,)), dma((20,)), dma((16,)), dma((16,)),
        dma((16,)), dma((16,)), dma((4,)), dma((4,)),
        dma((16,)), dma((16,)), dma((13,)), dma((2, 6)), dma((2,)), dma((5,)),
    ]
    res = pl.pallas_call(
        kernel,
        out_shape=out_shape,
        in_specs=[hbm] * 5 + [pl.BlockSpec(memory_space=pltpu.VMEM)] * 2,
        out_specs=[hbm] * len(out_shape),
        scratch_shapes=scratch,
        compiler_params=pltpu.CompilerParams(
            collective_id=0, has_side_effects=True, vmem_limit_bytes=63 * 1024 * 1024
        ),
    )(tokens, grad_out, w_gate, w_up, w_down, expert_ids.T, gate_prob.T)
    block = pl.BlockSpec
    return pl.pallas_call(
        finish,
        grid=(4,),
        out_shape=(
            sds((TOK, D), BF),
            sds((TOK, D), BF),
            sds((2, 512, FF), BF),
            sds((2, 512, FF), BF),
            sds((2, FF, 512), BF),
        ),
        in_specs=[
            block((2, 32, D), lambda i: (0, i, 0)),
            block((2, 128, 2 * FF), lambda i: (0, i, 0)),
            block((2, 96, 512), lambda i: (0, i, 0)),
            block((2, 2, 128, 2 * FF), lambda i: (0, 0, i, 0)),
            block((2, 2, 96, 512), lambda i: (0, 0, i, 0)),
            block((2, 2, 32, D), lambda i: (0, 0, i, 0)),
        ],
        out_specs=(
            block((32, D), lambda i: (i, 0)),
            block((32, D), lambda i: (i, 0)),
            block((2, 128, FF), lambda i: (0, i, 0)),
            block((2, 128, FF), lambda i: (0, i, 0)),
            block((2, 96, 512), lambda i: (0, i, 0)),
        ),
        compiler_params=pltpu.CompilerParams(vmem_limit_bytes=63 * 1024 * 1024),
    )(res[0].reshape(2, TOK, D), *res[1:5], res[5].reshape(2, 2, TOK, D))


def solution(mesh):
    return jax.shard_map(
        per_device,
        mesh=mesh,
        in_specs=(
            P(("expert", "dp"), None),
            P(("expert", "dp"), None),
            P(("expert", "dp"), None),
            P("expert", "dp", None),
            P("expert", "dp", None),
            P("expert", None, "dp"),
            P(("expert", "dp"), None),
        ),
        out_specs=(
            P(("expert", "dp"), None),
            P(("expert", "dp"), None),
            P("expert", "dp", None),
            P("expert", "dp", None),
            P("expert", None, "dp"),
        ),
        check_vma=False,
    )
```

```python
import jax
import jax.numpy as jnp
from jax import lax
from jax.experimental import pallas as pl
from jax.experimental.pallas import tpu as pltpu
from jax.sharding import PartitionSpec as P

MESH = pl.DeviceIdType.MESH
BF = jnp.bfloat16
F32 = jnp.float32
D = 2048
FF = 384
TOK = 128
CAP = 24
KEEP = {"S": 6, "P": 6, "Q": 12, "Z": 8}
ROWS = 768
XW = D + 128
PLACES = [
    (0, 0), (0, 1), (0, 3), (1, 0), (3, 0), (0, 2), (2, 0),
    (2, 1), (2, 3), (1, 2), (3, 2), (2, 2),
    (1, 1), (1, 3), (3, 1), (3, 3),
]
NT = (((1,), (1,)), ((), ()))
TN = (((0,), (0,)), ((), ()))
NN = (((1,), (0,)), ((), ()))


def dot(a, b, dims):
    return lax.dot_general(a, b, dims, preferred_element_type=F32)


def kernel(
    tok, g, wgate, wup, wdown, eids, gprob,
    own_r, own_gu, own_d, zfg, zfd, pfull,
    xbuf, gbuf, ysib, qopp, qfull, popp,
    S, L, Wgu, Wd, YD, H, DAB, PW, P4, MB, MT, YL, RB, zhg, zhd, early,
    a_send, a_recv, s_send, s_recv, w_send, w_recv, y_send, y_recv,
    q_send, q_recv, p_send, p_recv, z_send, z_recv, loc, ld, yl_sem, m_send,
):
    me = lax.axis_index("expert")
    z = lax.axis_index("dp")
    c = lax.rem(me, 2)
    x = lax.rem(me // 2, 4)
    y = me // 8
    sib = {"expert": me + 1 - 2 * c}
    zr, zl, zo = lax.rem(z + 1, 4), lax.rem(z + 3, 4), lax.rem(z + 2, 4)

    def pq(dp, dq):
        dx = dp + c * (dq - dp)
        dy = dq + c * (dp - dq)
        return {"expert": (lax.rem(y + dy, 4) * 4 + lax.rem(x + dx, 4)) * 2 + c}

    dev = {"P+": pq(1, 0), "P-": pq(3, 0), "Q+": pq(0, 1), "Q-": pq(0, 3), "S": sib, "Z+": {"dp": zr}, "Z-": {"dp": zl}}

    def slot(dp, dq):
        k0, k1 = PLACES.index((dp, dq)), PLACES.index((dq, dp))
        return k0 + c * (k1 - k0)

    barrier = pltpu.get_barrier_semaphore()
    for d in dev.values():
        pl.semaphore_signal(barrier, inc=1, device_id=d, device_id_type=MESH)

    flying = {}

    def send(src, dst, ssem, rsem, to):
        cp = pltpu.make_async_remote_copy(
            src_ref=src, dst_ref=dst, send_sem=ssem, recv_sem=rsem, device_id=dev[to], device_id_type=MESH
        )
        line = flying.setdefault(to[0], [])
        while len(line) >= KEEP[to[0]]:
            line.pop(0).wait_send()
        cp.start()
        line.append(cp)

    def arrived(dst, ssem, rsem):
        pltpu.make_async_remote_copy(
            src_ref=dst, dst_ref=dst, send_sem=ssem, recv_sem=rsem, device_id=dev["S"], device_id_type=MESH
        ).wait_recv()

    half = pl.ds(pl.multiple_of(c * TOK, TOK), TOK)
    other = pl.ds(pl.multiple_of((1 - c) * TOK, TOK), TOK)
    bufs = (xbuf, gbuf)
    counts = {"a": 0, "m": 0}

    def nxt(name):
        counts[name] += 1
        return counts[name] - 1

    def aidx(dp, dq, k):
        return (dp * 4 + dq) * 2 + k

    def blk(dp, dq, k):
        return bufs[k].at[slot(dp, dq), half, :]

    def push(dp, dq, k, to):
        ddp, ddq = dp, dq
        if to == "P+":
            ddp = (dp + 3) % 4
        elif to == "P-":
            ddp = (dp + 1) % 4
        elif to == "Q+":
            ddq = (dq + 3) % 4
        elif to == "Q-":
            ddq = (dq + 1) % 4
        launch(dp, dq, k, slot(ddp, ddq), a_send, nxt("a"), a_recv.at[aidx(ddp, ddq, k)], to)

    def launch(dp, dq, k, r, ssem, i, rsem, to):
        dst = bufs[k].at[r, half, :]
        if dp or dq:
            send(blk(dp, dq, k), dst, ssem.at[i], rsem, to)
        elif k == 1:
            send(g, dst, ssem.at[i], rsem, to)
        else:
            send(tok, bufs[0].at[r, half, pl.ds(0, D)], ssem.at[i], rsem, to)
            send(MT, bufs[0].at[r, half, pl.ds(D, 128)], m_send.at[counts["m"]], rsem, to)
            counts["m"] += 1

    def push_sib(dp, dq, k):
        i = aidx(dp, dq, k)
        launch(dp, dq, k, slot(dp, dq), s_send, i, s_recv.at[i], "S")

    def take(dp, dq, k):
        i = aidx(dp, dq, k)
        arrived(bufs[k].at[slot(dp, dq), half, :], a_send.at[0], a_recv.at[i])

    def take_sib(dp, dq, k):
        i = aidx(dq, dp, k)
        arrived(bufs[k].at[slot(dp, dq), other, :], s_send.at[0], s_recv.at[i])

    prob_in = gprob[...]
    hi = prob_in.astype(BF)
    mid = (prob_in - hi.astype(F32)).astype(BF)
    low = (prob_in - hi.astype(F32) - mid.astype(F32)).astype(BF)
    meta = [eids[...].astype(F32), hi.astype(F32), mid.astype(F32), low.astype(F32), jnp.zeros((96, TOK), F32)]
    MT[...] = jnp.concatenate(meta, axis=0).astype(BF)
    pl.semaphore_wait(barrier, 7)

    def zrows(i):
        return pl.ds(pl.multiple_of(i * 512, 512), 512)

    wsrc = (wgate, wup, wdown)

    def wdst(e, k, i):
        if k == 2:
            return Wd.at[e, i]
        return Wgu.at[e, zrows(i), pl.ds(k * FF, FF)]

    own_w = [
        pltpu.make_async_copy(wsrc[k].at[e], wdst(e, k, z), loc.at[5 + 3 * e + k]) for e in range(2) for k in range(3)
    ]

    def w_own(e, kinds=(0, 1, 2)):
        for k in kinds:
            for j, to in enumerate(("Z+", "Z-")):
                wsend(wsrc[k].at[e], wdst(e, k, z), e * 10 + 3 * j + k, to)

    def wsend(src, dst, i, to):
        send(src, dst, w_send.at[i], w_recv.at[i], to)

    def w_parts(e, i):
        lo = pl.ds(pl.multiple_of(i * 512, 512), 256)
        hi = pl.ds(pl.multiple_of(i * 512 + 256, 256), 256)
        return (Wgu.at[e, lo], Wgu.at[e, hi], Wd.at[e, i, pl.ds(0, 192)], Wd.at[e, i, pl.ds(192, 192)])

    def w_fwd(e):
        for k in range(3):
            arrived(wdst(e, k, zl), w_send.at[0], w_recv.at[e * 10 + k])
            arrived(wdst(e, k, zr), w_send.at[0], w_recv.at[e * 10 + 3 + k])
        for j in range(4):
            part = w_parts(e, (zl, zr)[j % 2])[j]
            wsend(part, part, e * 10 + 6 + j, ("Z+", "Z-")[j % 2])

    def w_last(e):
        for j in range(4):
            arrived(w_parts(e, zo)[j], w_send.at[0], w_recv.at[e * 10 + 6 + j])

    for k in range(2):
        push(0, 0, k, "P+")
        push(0, 0, 1 - k, "P-")
        push(0, 0, k, "Q+")
        push(0, 0, 1 - k, "Q-")
        if k == 0:
            w_own(0)
            w_own(1, (0,))
    push_sib(0, 0, 0)
    push_sib(0, 0, 1)
    for cp in own_w:
        cp.start()

    tri = (
        lax.broadcasted_iota(jnp.int32, (TOK, TOK), 0) <= lax.broadcasted_iota(jnp.int32, (TOK, TOK), 1)
    ).astype(F32).astype(BF)
    row8 = lax.broadcasted_iota(jnp.int32, (8, TOK), 0)
    slot_row = lax.broadcasted_iota(jnp.int32, (2 * CAP, TOK), 0).astype(F32)
    cf = c.astype(F32)
    e_own = (2 * me).astype(F32)
    e_sib = (2 * (me + 1 - 2 * c)).astype(F32)

    def load(chip, b, buf):
        r = 0 if chip == (0, 0) else slot(*chip)
        for cp in load_copies(r, b, buf):
            cp.start()

    def load_copies(r, b, buf):
        if isinstance(r, int):
            r0 = b * 512
            mine, theirs = pl.ds(pl.multiple_of(r0 + c * TOK, TOK), TOK), pl.ds(pl.multiple_of(r0 + TOK - c * TOK, TOK), TOK)
            mine_g = pl.ds(pl.multiple_of(r0 + 256 + c * TOK, TOK), TOK)
            theirs_g = pl.ds(pl.multiple_of(r0 + 256 + TOK - c * TOK, TOK), TOK)
            few = pl.ds(pl.multiple_of((1 - c) * TOK, TOK), 32)
            return (
                pltpu.make_async_copy(tok, buf.at[mine, :], ld.at[b, 0]),
                pltpu.make_async_copy(xbuf.at[0, other, pl.ds(0, D)], buf.at[theirs, :], ld.at[b, 1]),
                pltpu.make_async_copy(g, buf.at[mine_g, :], ld.at[b, 2]),
                pltpu.make_async_copy(gbuf.at[0, other, :], buf.at[theirs_g, :], ld.at[b, 3]),
                pltpu.make_async_copy(MT.at[pl.ds(0, 32), :], MB.at[b, c], ld.at[b, 4]),
                pltpu.make_async_copy(xbuf.at[0, few, pl.ds(D, 128)], MB.at[b, 1 - c], ld.at[b, 5]),
            )
        return (
            pltpu.make_async_copy(xbuf.at[r, :, pl.ds(0, D)], buf.at[pl.ds(b * 512, 256), :], ld.at[b, 0]),
            pltpu.make_async_copy(gbuf.at[r], buf.at[pl.ds(b * 512 + 256, 256), :], ld.at[b, 1]),
            pltpu.make_async_copy(xbuf.at[r, pl.ds(0, 32), pl.ds(D, 128)], MB.at[b, 0], ld.at[b, 2]),
            pltpu.make_async_copy(xbuf.at[r, pl.ds(TOK, 32), pl.ds(D, 128)], MB.at[b, 1], ld.at[b, 3]),
        )

    def pick(chip, b, buf):
        r = 0 if chip == (0, 0) else slot(*chip)
        for cp in load_copies(r, b, buf):
            cp.wait()
        ids, prob = [], []
        for t in range(2):
            ids.append(MB[b, t, 0:8].astype(F32))
            prob.append(
                MB[b, t, 8:16].astype(F32) + (MB[b, t, 16:24].astype(F32) + MB[b, t, 24:32].astype(F32))
            )
        ids_c = jnp.where(c == 0, ids[0], ids[1])
        todo = [(ids[0], e_own), (ids[1], e_own), (ids[0], e_own + 1), (ids[1], e_own + 1), (ids_c, e_sib), (ids_c, e_sib + 1)]
        hit = jnp.zeros((8, TOK), F32)
        pv = []
        for j, (idv, e) in enumerate(todo):
            m = jnp.where(idv == e, 1.0, 0.0)
            if j < 4:
                pv.append(jnp.sum(m * prob[j % 2], axis=0, keepdims=True))
            hit = jnp.where(row8 == j, jnp.sum(m, axis=0, keepdims=True), hit)
        rank = dot(hit.astype(BF), tri, NN)
        key = jnp.where(hit > 0.5, rank - 1.0, -1000.0)
        p256, pown, psib = [], [], []
        for e in range(2):
            p0 = jnp.where(key[2 * e : 2 * e + 1] == slot_row, 1.0, 0.0)
            p1 = jnp.where(key[2 * e + 1 : 2 * e + 2] + CAP == slot_row, 1.0, 0.0)
            w = jnp.sum(p0 * pv[2 * e] + p1 * pv[2 * e + 1], axis=1, keepdims=True)
            at = pl.ds(pl.multiple_of(e * ROWS + r * 48, 16), 48)
            PW[at, :] = jnp.broadcast_to(w, (48, 128))
            p256.append(jnp.concatenate([p0, p1], axis=1))
            pown.append(jnp.where(c == 0, p0, p1))
            psib.append(jnp.where(key[4 + e : 5 + e] + CAP * cf == slot_row, 1.0, 0.0))
        P4[r] = jnp.concatenate(pown + psib, axis=0).astype(BF)
        pick_m = jnp.concatenate(p256, axis=0).astype(BF)

        def cols(n, _):
            cc = pl.ds(pl.multiple_of(n * 1024, 1024), 1024)
            for t in range(2):
                src = buf[pl.ds(b * 512 + t * 256, 256), cc]
                got = dot(pick_m, src, NN).astype(BF)
                for e in range(2):
                    at = pl.ds(pl.multiple_of(t * 2 * ROWS + e * ROWS + r * 48, 16), 48)
                    S[at, cc] = got[e * 48 : e * 48 + 48]
            return 0

        lax.fori_loop(0, 2, cols, 0)

    def picks(some, buf):
        for i, chip in enumerate(some):
            for j in (i, i + 1):
                if j < len(some) and (j > i or i == 0):
                    for k in range(2):
                        take_sib(*some[j], k)
                    load(some[j], j % 2, buf)
            pick(chip, i % 2, buf)

    def forward(e, tile):
        first, n = tile
        lo, cnt = first * 48, n * 48
        xs = S[e * ROWS + lo : e * ROWS + lo + cnt, :]
        ab = dot(xs, Wgu[e], NN)
        g0 = (2 + e) * ROWS + lo
        dh = dot(S[g0 : g0 + cnt, 0:512], Wd[e, 0], NT)
        for i in range(1, 4):
            dh = dh + dot(S[g0 : g0 + cnt, i * 512 : i * 512 + 512], Wd[e, i], NT)
        w = PW[e * ROWS + lo : e * ROWS + lo + cnt, 0:1]
        a, b = ab[:, :FF], ab[:, FF:]
        s = 1.0 / (1.0 + jnp.exp(-a))
        act = a * s
        dh = dh * w
        H[e, lo : lo + cnt, :] = (act * b * w).astype(BF)
        DAB[e, lo : lo + cnt, 0:FF] = (dh * b * s * (1.0 + a * (1.0 - s))).astype(BF)
        DAB[e, lo : lo + cnt, FF:] = (dh * act).astype(BF)

    def outputs(e, tile):
        first, n = tile
        lo, cnt = first * 48, n * 48
        for i in range(4):
            yv = dot(H[e, lo : lo + cnt, :], Wd[e, i], NN).astype(BF)
            YD[first : first + n, e * 48 : e * 48 + 48, i * 512 : i * 512 + 512] = yv.reshape(n, 48, 512)
        for i in range(4):
            dv = dot(DAB[e, lo : lo + cnt, :], Wgu[e, i * 512 : i * 512 + 512, :], NT).astype(BF)
            YD[first : first + n, e * 48 : e * 48 + 48, D + i * 512 : D + i * 512 + 512] = dv.reshape(n, 48, 512)

    def weight_grads(e):
        def part(j, _):
            i = lax.rem(z + j, 4)
            cc = zrows(i)
            xs = S[e * ROWS : e * ROWS + ROWS, cc]
            gs = S[(2 + e) * ROWS : (3 + e) * ROWS, cc]
            Wgu[e, cc, :] = dot(xs, DAB[e], TN).astype(BF)
            Wd[e, i] = dot(H[e], gs, TN).astype(BF)
            return 0

        lax.fori_loop(2, 3, part, 0)
        z_first(e)
        lax.fori_loop(3, 6, part, 0)

    def zsend(src, dst, i, to):
        send(src, dst, z_send.at[i], z_recv.at[i], to)

    def z_first(e):
        base = e * 8
        lo = pl.ds(pl.multiple_of(zo * 512, 512), 256)
        hi = pl.ds(pl.multiple_of(zo * 512 + 256, 256), 256)
        zsend(Wgu.at[e, lo], zhg.at[e, 0], base + 0, "Z+")
        zsend(Wgu.at[e, hi], zhg.at[e, 1], base + 1, "Z-")
        zsend(Wd.at[e, zo, pl.ds(0, 192)], zhd.at[e, 0], base + 2, "Z+")
        zsend(Wd.at[e, zo, pl.ds(192, 192)], zhd.at[e, 1], base + 3, "Z-")

    def z_second(e):
        base = e * 8
        for i, (dst, rows) in enumerate(((zhg.at[e, 0], 0), (zhg.at[e, 1], 0), (zhd.at[e, 0], 0), (zhd.at[e, 1], 0))):
            arrived(dst, z_send.at[0], z_recv.at[base + i])

        def add(j, _):
            for i, (zz, off) in enumerate(((zr, 0), (zl, 256))):
                at = pl.ds(pl.multiple_of(zz * 512 + off + j * 32, 32), 32)
                Wgu[e, at, :] = (Wgu[e, at, :].astype(F32) + zhg[e, i, pl.ds(j * 32, 32), :].astype(F32)).astype(BF)
            return 0

        lax.fori_loop(0, 8, add, 0)

        def add_d(j, _):
            for i, (zz, off) in enumerate(((zr, 0), (zl, 192))):
                at = pl.ds(pl.multiple_of(off + j * 32, 32), 32)
                Wd[e, zz, at, :] = (Wd[e, zz, at, :].astype(F32) + zhd[e, i, pl.ds(j * 32, 32), :].astype(F32)).astype(BF)
            return 0

        lax.fori_loop(0, 6, add_d, 0)
        zsend(Wgu.at[e, zrows(zr)], zfg.at[e, 0], base + 4, "Z+")
        zsend(Wgu.at[e, zrows(zl)], zfg.at[e, 1], base + 5, "Z-")
        zsend(Wd.at[e, zr], zfd.at[e, 0], base + 6, "Z+")
        zsend(Wd.at[e, zl], zfd.at[e, 1], base + 7, "Z-")

    outs = []

    def z_third(e):
        base = e * 8
        for i, dst in enumerate((zfg.at[e, 0], zfg.at[e, 1], zfd.at[e, 0], zfd.at[e, 1])):
            arrived(dst, z_send.at[0], z_recv.at[base + 4 + i])

    def z_own(e):
        for i, (src, dst) in enumerate(((Wgu.at[e, zrows(z)], own_gu.at[e]), (Wd.at[e, z], own_d.at[e]))):
            cp = pltpu.make_async_copy(src, dst, loc.at[e * 2 + i])
            cp.start()
            outs.append(cp)

    far = [(2, 2), (1, 2), (3, 2), (0, 2)]
    near = [(2, 1), (2, 3), (0, 1), (0, 3), (1, 1), (1, 3), (3, 1), (3, 3)]
    mine = [(2, 0), (1, 0), (3, 0), (0, 0)]
    chips = far + near + mine

    def yd_sends(some):
        for i, (dp, dq) in enumerate(chips):
            if (dp, dq) in some:
                r = slot(dq, dp)
                send(YD.at[r], ysib.at[r], y_send.at[i], y_recv.at[i], "S")

    def yd_load(i):
        r = slot(*chips[i])
        return pltpu.make_async_copy(ysib.at[r], YL.at[i % 2], yl_sem.at[i % 2])

    def yd_start(i):
        r = slot(*chips[i])
        arrived(ysib.at[r], y_send.at[0], y_recv.at[i])
        yd_load(i).start()

    def cblk(dp, dq, k=0, n=1):
        if dq == 2:
            return L, dp * 256 + k * 128, n * 128
        if dp in (0, 2) and dq:
            return early, dp * 256 + dq // 2 * 256 + k * 128, n * 128
        return S, dp * 768 + {0: 0, 1: 256, 3: 512}[dq] + k * 128, n * 128

    def cref(dp, dq, k=0, n=1):
        ref, row, cnt = cblk(dp, dq, k, n)
        return ref.at[pl.ds(row, cnt), :]

    def combine(dp, dq, ahead=True):
        i = chips.index((dp, dq))
        if i + 1 < 16 and ahead:
            yd_start(i + 1)
        yd_load(i).wait()
        r = slot(dp, dq)
        ref, row, _ = cblk(dp, dq)
        pm = P4[r]

        def cols(n, _):
            cc = pl.ds(pl.multiple_of(n * 512, 512), 512)
            for k in range(2):
                ck = pl.ds(pl.multiple_of(k * D + n * 512, 512), 512)
                rows = jnp.concatenate([YD[r, :, ck], YL[i % 2, :, ck]], axis=0)
                ref[row + k * 128 : row + k * 128 + 128, cc] = dot(pm, rows, TN).astype(BF)
            return 0

        lax.fori_loop(0, 4, cols, 0)

    def fetch(pairs):
        cps = [pltpu.make_async_copy(s, d, ld.at[0, i]) for i, (s, d) in enumerate(pairs)]
        for cp in cps:
            cp.start()
        for cp in cps:
            cp.wait()

    def accumulate(dp, dq, k, n, parts):
        ref, row, cnt = cblk(dp, dq, k, n)

        def add(j, _):
            at = pl.ds(pl.multiple_of(row + j * 16, 16), 16)
            total = ref[at, :].astype(F32)
            for off in parts:
                total = total + RB[pl.ds(pl.multiple_of(off + j * 16, 16), 16), :].astype(F32)
            ref[at, :] = total.astype(BF)
            return 0

        lax.fori_loop(0, cnt // 16, add, 0)

    def qsend(src, dst, dp, j, to):
        send(src, dst, q_send.at[dp * 4 + j], q_recv.at[dp * 4 + j], to)

    def q_first(dp):
        qsend(cref(dp, 2, 0), qopp.at[dp, 0], dp, 0, "Q+")
        qsend(cref(dp, 2, 1), qopp.at[dp, 1], dp, 1, "Q-")

    def q_second(dp):
        arrived(qopp.at[dp, 0], q_send.at[0], q_recv.at[dp * 4 + 0])
        arrived(qopp.at[dp, 1], q_send.at[0], q_recv.at[dp * 4 + 1])
        fetch([(qopp.at[dp, 0], RB.at[pl.ds(512, 128)]), (qopp.at[dp, 1], RB.at[pl.ds(640, 128)])])
        accumulate(dp, 1, 0, 1, (512,))
        qsend(cref(dp, 1, 0, 2), qfull.at[dp, 0], dp, 2, "Q+")
        accumulate(dp, 3, 1, 1, (640,))
        qsend(cref(dp, 3, 0, 2), qfull.at[dp, 1], dp, 3, "Q-")

    def psend(src, dst, j, to):
        send(src, dst, p_send.at[j], p_recv.at[j], to)

    def q_third(dp):
        arrived(qfull.at[dp, 0], q_send.at[0], q_recv.at[dp * 4 + 2])
        arrived(qfull.at[dp, 1], q_send.at[0], q_recv.at[dp * 4 + 3])
        fetch([(qfull.at[dp, 0], RB.at[pl.ds(0, 256)]), (qfull.at[dp, 1], RB.at[pl.ds(256, 256)])])
        accumulate(dp, 0, 0, 2, (0, 256))
        if dp == 2:
            psend(cref(2, 0, 0), popp.at[0], 0, "P+")
            psend(cref(2, 0, 1), popp.at[1], 1, "P-")
        elif dp == 1:
            arrived(popp.at[0], p_send.at[0], p_recv.at[0])
            fetch([(popp.at[0], RB.at[pl.ds(512, 128)])])
            accumulate(1, 0, 0, 1, (512,))
            psend(cref(1, 0, 0, 2), pfull.at[0], 2, "P+")
        elif dp == 3:
            arrived(popp.at[1], p_send.at[0], p_recv.at[1])
            fetch([(popp.at[1], RB.at[pl.ds(512, 128)])])
            accumulate(3, 0, 1, 1, (512,))
            psend(cref(3, 0, 0, 2), pfull.at[1], 3, "P-")
        else:
            cp = pltpu.make_async_copy(cref(0, 0, 0, 2), own_r, loc.at[4])
            cp.start()
            outs.append(cp)
            arrived(pfull.at[0], p_send.at[0], p_recv.at[2])
            arrived(pfull.at[1], p_send.at[0], p_recv.at[3])

    T0, T1, T2 = (0, 7), (7, 5), (12, 4)
    take(3, 0, 0)
    push(3, 0, 0, "P+")
    take(1, 0, 1)
    push(1, 0, 1, "P-")
    take(0, 3, 0)
    push(0, 3, 0, "Q+")
    take(0, 1, 1)
    push(0, 1, 1, "Q-")
    push(3, 0, 0, "Q+")
    push(1, 0, 1, "Q-")
    take(1, 0, 0)
    push(1, 0, 0, "Q+")
    take(3, 0, 1)
    push(3, 0, 1, "Q-")
    take(0, 1, 0)
    take(0, 3, 1)
    for chip in ((1, 0), (3, 0), (0, 1), (0, 3)):
        for k in range(2):
            push_sib(*chip, k)
    w_fwd(0)
    w_own(1, (1, 2))
    picks([(0, 0)], L)
    for k in range(2):
        take(2, 0, k)
    push(2, 0, 0, "Q+")
    push(2, 0, 1, "Q-")
    push(2, 0, 0, "Q-")
    push(2, 0, 1, "Q+")
    for k in range(2):
        push_sib(2, 0, k)
        take(0, 2, k)
        push_sib(0, 2, k)
    picks([(0, 1), (0, 3), (1, 0), (3, 0)], L)
    for dp in (3, 1):
        take(dp, 3, 0)
        push(dp, 3, 0, "Q+")
        take(dp, 1, 1)
        push(dp, 1, 1, "Q-")
    for dp in (3, 1):
        push_sib(dp, 3, 0)
        push_sib(dp, 1, 1)
    picks([(0, 2), (2, 0)], L)
    take(2, 3, 0)
    push(2, 3, 0, "Q+")
    take(2, 1, 1)
    push(2, 1, 1, "Q-")
    for dp in (3, 1):
        push(dp, 0, 0, "Q-")
        push(dp, 0, 1, "Q+")
    take(2, 1, 0)
    take(2, 3, 1)
    for chip in ((2, 1), (2, 3)):
        for k in range(2):
            push_sib(*chip, k)
    w_last(0)
    for cp in own_w:
        cp.wait()
    forward(0, T0)
    outputs(0, T0)
    for dp in (3, 1):
        for k in range(2):
            take(dp, 2, k)
            push_sib(dp, 2, k)
    w_fwd(1)
    picks([(2, 1), (2, 3), (1, 2), (3, 2)], L)
    for k in range(2):
        take(2, 2, k)
        push_sib(2, 2, k)
    picks([(2, 2)], L)
    forward(0, T1)
    outputs(0, T1)
    w_last(1)
    forward(1, T1)
    outputs(1, T1)
    yd_sends([(2, 2), (1, 2), (3, 2), (2, 1), (2, 3)])
    forward(1, T0)
    outputs(1, T0)
    yd_sends([(0, 2), (0, 1), (0, 3), (2, 0), (1, 0), (3, 0), (0, 0)])
    yd_start(0)
    for dp, dq in far:
        combine(dp, dq)
        q_first(dp)
    combine(2, 1)
    combine(2, 3)
    for dp in (3, 1):
        take(dp, 1, 0)
        push_sib(dp, 1, 0)
        take(dp, 3, 1)
        push_sib(dp, 3, 1)
    picks([(1, 1), (1, 3), (3, 1), (3, 3)], RB)
    q_second(2)
    forward(0, T2)
    outputs(0, T2)
    for cp in flying["Z"]:
        cp.wait_send()
    flying["Z"] = []
    weight_grads(0)
    combine(0, 1)
    combine(0, 3, False)
    forward(1, T2)
    outputs(1, T2)
    yd_sends([(1, 1), (1, 3), (3, 1), (3, 3)])
    yd_start(8)
    q_second(0)
    weight_grads(1)
    z_own(0)
    z_own(1)
    combine(1, 1)
    combine(1, 3)
    q_second(1)
    z_second(0)
    combine(3, 1)
    combine(3, 3)
    q_second(3)
    z_second(1)
    combine(2, 0)
    q_third(2)
    for dp, dq in mine[1:]:
        combine(dp, dq)
    q_third(1)
    q_third(3)
    z_third(0)
    q_third(0)
    z_third(1)
    for cp in outs:
        cp.wait()
    for line in flying.values():
        for cp in line:
            cp.wait_send()


def finish(own_r, own_gu, own_d, zfg, zfd, pfull, mixed, gtok, ggate, gup, gdown):
    for k, out in enumerate((mixed, gtok)):
        out[...] = (own_r[k].astype(F32) + pfull[0, k].astype(F32) + pfull[1, k].astype(F32)).astype(BF)
    for e in range(2):
        gu = (own_gu[e].astype(F32) + zfg[e, 0].astype(F32) + zfg[e, 1].astype(F32)).astype(BF)
        ggate[e] = gu[:, :FF]
        gup[e] = gu[:, FF:]
        gdown[e] = (own_d[e].astype(F32) + zfd[e, 0].astype(F32) + zfd[e, 1].astype(F32)).astype(BF)


def per_device(tokens, expert_ids, gate_prob, w_gate, w_up, w_down, grad_out):
    sds = jax.ShapeDtypeStruct
    hbm = pl.BlockSpec(memory_space=pl.ANY)
    dma = pltpu.SemaphoreType.DMA
    out_shape = (
        sds((256, D), BF),
        sds((2, 512, 2 * FF), BF),
        sds((2, FF, 512), BF),
        sds((2, 2, 512, 2 * FF), BF),
        sds((2, 2, FF, 512), BF),
        sds((2, 256, D), BF),
        sds((16, 256, XW), BF),
        sds((16, 256, D), BF),
        sds((16, 96, 2 * D), BF),
        sds((4, 2, TOK, D), BF),
        sds((4, 2, 256, D), BF),
        sds((2, TOK, D), BF),
    )
    scratch = [
        pltpu.VMEM((4 * ROWS, D), BF),
        pltpu.VMEM((1024, D), BF),
        pltpu.VMEM((2, D, 2 * FF), BF),
        pltpu.VMEM((2, 4, FF, 512), BF),
        pltpu.VMEM((16, 96, 2 * D), BF),
        pltpu.VMEM((2, ROWS, FF), BF),
        pltpu.VMEM((2, ROWS, 2 * FF), BF),
        pltpu.VMEM((2 * ROWS, 128), F32),
        pltpu.VMEM((16, 192, TOK), BF),
        pltpu.VMEM((2, 2, 32, 128), BF),
        pltpu.VMEM((128, 128), BF),
        pltpu.VMEM((2, 96, 2 * D), BF),
        pltpu.VMEM((1024, D), BF),
        pltpu.VMEM((2, 2, 256, 2 * FF), BF),
        pltpu.VMEM((2, 2, 192, 512), BF),
        pltpu.VMEM((1024, D), BF),
        dma((30,)), dma((32,)), dma((32,)), dma((32,)),
        dma((20,)), dma((20,)), dma((16,)), dma((16,)),
        dma((16,)), dma((16,)), dma((4,)), dma((4,)),
        dma((16,)), dma((16,)), dma((13,)), dma((2, 6)), dma((2,)), dma((5,)),
    ]
    res = pl.pallas_call(
        kernel,
        out_shape=out_shape,
        in_specs=[hbm] * 5 + [pl.BlockSpec(memory_space=pltpu.VMEM)] * 2,
        out_specs=[hbm] * len(out_shape),
        scratch_shapes=scratch,
        compiler_params=pltpu.CompilerParams(
            collective_id=0, has_side_effects=True, vmem_limit_bytes=63 * 1024 * 1024
        ),
    )(tokens, grad_out, w_gate, w_up, w_down, expert_ids.T, gate_prob.T)
    block = pl.BlockSpec
    return pl.pallas_call(
        finish,
        grid=(4,),
        out_shape=(
            sds((TOK, D), BF),
            sds((TOK, D), BF),
            sds((2, 512, FF), BF),
            sds((2, 512, FF), BF),
            sds((2, FF, 512), BF),
        ),
        in_specs=[
            block((2, 32, D), lambda i: (0, i, 0)),
            block((2, 128, 2 * FF), lambda i: (0, i, 0)),
            block((2, 96, 512), lambda i: (0, i, 0)),
            block((2, 2, 128, 2 * FF), lambda i: (0, 0, i, 0)),
            block((2, 2, 96, 512), lambda i: (0, 0, i, 0)),
            block((2, 2, 32, D), lambda i: (0, 0, i, 0)),
        ],
        out_specs=(
            block((32, D), lambda i: (i, 0)),
            block((32, D), lambda i: (i, 0)),
            block((2, 128, FF), lambda i: (0, i, 0)),
            block((2, 128, FF), lambda i: (0, i, 0)),
            block((2, 96, 512), lambda i: (0, i, 0)),
        ),
        compiler_params=pltpu.CompilerParams(vmem_limit_bytes=63 * 1024 * 1024),
    )(res[0].reshape(2, TOK, D), *res[1:5], res[5].reshape(2, 2, TOK, D))


def solution(mesh):
    return jax.shard_map(
        per_device,
        mesh=mesh,
        in_specs=(
            P(("expert", "dp"), None),
            P(("expert", "dp"), None),
            P(("expert", "dp"), None),
            P("expert", "dp", None),
            P("expert", "dp", None),
            P("expert", None, "dp"),
            P(("expert", "dp"), None),
        ),
        out_specs=(
            P(("expert", "dp"), None),
            P(("expert", "dp"), None),
            P("expert", "dp", None),
            P("expert", "dp", None),
            P("expert", None, "dp"),
        ),
        check_vma=False,
    )
```
